256 devices in a mesh: blk: 64 (over z_lo, y, x), uly: 4 (over z_hi, core).
Axes of the slice: x: 4, y: 4, z: 8 (z_hi: 2, z_lo: 4; z = z_hi * 4 + z_lo), core: 2. Of those that a mesh axis runs over, the one named last changes fastest.
Arguments:
- video_q: bfloat16 [16384, 3072], P(('blk', 'uly')), may hold values from -6 to 6
- video_k: bfloat16 [16384, 3072], P(('blk', 'uly')), may hold values from -7 to 7
- video_v: bfloat16 [16384, 3072], P(('blk', 'uly')), may hold values from -6 to 6
- text_q: bfloat16 [256, 3072], P('blk', 'uly'), may hold values from -6 to 6
- text_k: bfloat16 [256, 3072], P('blk', 'uly'), may hold values from -6 to 6
- text_v: bfloat16 [256, 3072], P('blk', 'uly'), may hold values from -6 to 6
- video_q_gain: float32 [128], replicated, may hold values from 0.7 to 4, as said below
- video_k_gain: float32 [128], replicated, may hold values from 0.7 to 4, as said below
- text_q_gain: float32 [128], replicated, may hold values from 0.7 to 4, as said below
- text_k_gain: float32 [128], replicated, may hold values from 0.7 to 4, as said below
- frame_ids: int32 [16384], P(('blk', 'uly')), may hold values from 0 to 32, as said below
- row_ids: int32 [16384], P(('blk', 'uly')), may hold values from 0 to 44, as said below
- col_ids: int32 [16384], P(('blk', 'uly')), may hold values from 0 to 79, as said below
- text_mask: int32 [256], P('blk'), may hold values from 0 to 1, as said below
Outputs:
- video_out: bfloat16 [16384, 3072], P(('blk', 'uly'))
- text_out: bfloat16 [256, 3072], P('blk', 'uly')
The draws below stay inside these ranges and needn't reach their ends.
Inputs may be any that keep to these rules, and one draw needn't show every extreme that they name: `video_q_gain`: positive gains. `video_k_gain`: positive gains. `text_q_gain`: positive gains. `text_k_gain`: positive gains. `frame_ids`: each token's (frame, row, column) is one cell of a clip of 33 frames of 45 x 80 cells, different for every token; every frame holds some tokens. `row_ids`: see frame_ids. `col_ids`: see frame_ids. `text_mask`: a leading run of ones of 64 or more tokens, then zeros, at least one zero.
All inputs are finite; a program needn't handle non-finite values.
Results may differ from the reference program's by a relative error of at most 0.0085.
The reference program's roundings to bfloat16 on the way count: a program that leaves them out, or rounds other values in their place, can miss the bound.
Values may be sent and summed in bfloat16 or wider, within the bound.
No kernel may reach another device: no remote copies, remote signals or barrier semaphores. Data moves between devices by JAX's collectives and lax.ppermute only.
A program may use at most 192 MiB of HBM per device.

```python
import jax
import jax.numpy as jnp
from jax import lax

HEADS = 24
HD = 128
D = 3072
RT = 16
RH = 56
RW = 56
GRID_H = 45
GRID_W = 80
FRAMES = 33
TXT = 256
TOKENS = 16384


def shared_field(key):
    return jax.random.normal(key, (TOKENS, D), jnp.float32)


def draw_video_k(key, part):
    field = jnp.clip(shared_field(key), -6.0, 6.0)
    return field.astype(jnp.bfloat16)


def draw_video_q(key, part):
    key = jax.random.fold_in(key, 1)
    own = jnp.clip(jax.random.normal(key, (TOKENS, D), jnp.float32), -6.0, 6.0)
    return own.astype(jnp.bfloat16)


def gain_values(key, low, high):
    logs = jax.random.uniform(key, (HD,), jnp.float32, jnp.log(low), jnp.log(high))
    return jnp.exp(logs)


def draw_video_q_gain(key, part):
    key = jax.random.fold_in(key, 3)
    return gain_values(key, 0.7, 2.2)


def draw_video_k_gain(key, part):
    key = jax.random.fold_in(key, 4)
    return gain_values(key, 0.7, 2.2)


def draw_text_q_gain(key, part):
    key = jax.random.fold_in(key, 5)
    return gain_values(key, 0.7, 2.2)


def draw_text_k_gain(key, part):
    key = jax.random.fold_in(key, 6)
    return gain_values(key, 0.7, 2.2)


def grid_cells(key):
    order_key = jax.random.fold_in(key, 21)
    shift_key = jax.random.fold_in(key, 22)
    cells = GRID_H * GRID_W
    order = jax.random.permutation(order_key, TOKENS).astype(jnp.int32)
    frame = order % FRAMES
    within = order // FRAMES
    offsets = jax.random.randint(shift_key, (FRAMES,), 0, cells).astype(jnp.int32)
    offsets = jnp.where(jnp.arange(FRAMES) == 0, cells - 1, offsets).astype(jnp.int32)
    picked = jnp.sum(jnp.where(frame[:, None] == jnp.arange(FRAMES)[None, :], offsets[None, :], 0), axis=1).astype(jnp.int32)
    cell = (within + picked) % cells
    return (frame, cell)


def draw_frame_ids(key, part):
    frame, cell = grid_cells(key)
    return frame


def draw_row_ids(key, part):
    frame, cell = grid_cells(key)
    return cell // GRID_W


def draw_col_ids(key, part):
    frame, cell = grid_cells(key)
    return cell % GRID_W


def draw_text_mask(key, part):
    key = jax.random.fold_in(key, 9)
    count = jax.random.randint(key, (), TXT // 4, TXT)
    return (jnp.arange(TXT) < count).astype(jnp.int32)


def levels(rng, shape, pieces, low, high):
    level, own = 1.0, jax.random.fold_in(rng, 6)
    for dim, blocks in pieces:
        heights = jnp.exp(jax.random.uniform(jax.random.fold_in(own, dim), (blocks,), jnp.float32, low / len(pieces), high / len(pieces)))
        level = level * jnp.repeat(heights, shape[dim] // blocks).reshape([-1 if axis == dim else 1 for axis in range(len(shape))])
    return level


def normal_values(stream_key, shape, scale, reach, split=(), kind=jnp.bfloat16):
    values = scale * jax.random.normal(stream_key, shape, jnp.float32)
    if split:
        values = values * levels(stream_key, shape, split, -0.22, 0.18)
    return jnp.clip(values, -reach, reach).astype(kind)


def setup_inputs(seed: int = 0) -> dict:
    key_of = jax.random.split(jax.random.key(seed), 15)
    return {
        "video_q": draw_video_q(jax.random.fold_in(key_of[14], 71), 0),
        "video_k": draw_video_k(jax.random.fold_in(key_of[14], 71), 0),
        "video_v": normal_values(key_of[2], (TOKENS, D), 1.0, 6.0, ((0, 256),)),
        "text_q": normal_values(key_of[3], (TXT, D), 1.0, 6.0, ((0, 64), (1, 4))),
        "text_k": normal_values(key_of[4], (TXT, D), 1.0, 6.0, ((0, 64), (1, 4))),
        "text_v": normal_values(key_of[5], (TXT, D), 1.0, 6.0, ((0, 64), (1, 4))),
        "video_q_gain": draw_video_q_gain(jax.random.fold_in(key_of[14], 71), 0),
        "video_k_gain": draw_video_k_gain(jax.random.fold_in(key_of[14], 71), 0),
        "text_q_gain": draw_text_q_gain(jax.random.fold_in(key_of[14], 71), 0),
        "text_k_gain": draw_text_k_gain(jax.random.fold_in(key_of[14], 71), 0),
        "frame_ids": draw_frame_ids(jax.random.fold_in(key_of[14], 71), 0),
        "row_ids": draw_row_ids(jax.random.fold_in(key_of[14], 71), 0),
        "col_ids": draw_col_ids(jax.random.fold_in(key_of[14], 71), 0),
        "text_mask": draw_text_mask(jax.random.fold_in(key_of[14], 71), 0),
    }


def rotary_tables(frames, rows_pos, cols_pos):
    angles = []
    for width, position in ((RT, frames), (RH, rows_pos), (RW, cols_pos)):
        index = jnp.arange(width // 2).astype(jnp.float32)
        freqs = jnp.power(jnp.float32(256.0), -2.0 * index / width)
        angles.append(position.astype(jnp.float32)[:, None] * freqs[None, :])
    angle = jnp.concatenate(angles, axis=1)
    return (jnp.cos(angle), jnp.sin(angle))

def norm_heads(values, gain):
    heads_view = values.astype(jnp.float32).reshape(values.shape[0], -1, HD)
    meansq = lax.optimization_barrier(jnp.mean(heads_view * heads_view, axis=-1, keepdims=True))
    return heads_view * lax.rsqrt(meansq + 1e-06) * gain

def rotate(heads_view, cosine, sine):
    pairs = heads_view.reshape(heads_view.shape[0], heads_view.shape[1], HD // 2, 2)
    first = pairs[..., 0]
    second = pairs[..., 1]
    cos_b = cosine[:, None, :]
    sin_b = sine[:, None, :]
    turned = jnp.stack([first * cos_b - second * sin_b, first * sin_b + second * cos_b], axis=-1)
    return turned.reshape(heads_view.shape)

def attend_head(query_h, key_h, value_h, valid):
    scores = jnp.dot(query_h, key_h.T, preferred_element_type=jnp.float32) / jnp.sqrt(jnp.float32(HD))
    scores = jnp.where(valid[None, :], scores, -1e+30)
    largest = lax.optimization_barrier(jnp.max(scores, axis=-1, keepdims=True))
    expo = jnp.where(valid[None, :], jnp.exp(scores - largest), 0.0)
    total = lax.optimization_barrier(jnp.sum(expo, axis=-1, keepdims=True))
    mixed = jnp.dot(expo.astype(jnp.bfloat16), value_h, preferred_element_type=jnp.float32) / total
    return mixed.astype(jnp.bfloat16)

def reference(video_q, video_k, video_v, text_q, text_k, text_v, video_q_gain, video_k_gain, text_q_gain, text_k_gain, frame_ids, row_ids, col_ids, text_mask):
    cosine, sine = rotary_tables(frame_ids, row_ids, col_ids)
    rot_q = rotate(norm_heads(video_q, video_q_gain), cosine, sine).astype(jnp.bfloat16)
    rot_k = rotate(norm_heads(video_k, video_k_gain), cosine, sine).astype(jnp.bfloat16)
    norm_tq = norm_heads(text_q, text_q_gain).astype(jnp.bfloat16)
    norm_tk = norm_heads(text_k, text_k_gain).astype(jnp.bfloat16)
    queries = jnp.concatenate([rot_q, norm_tq], axis=0)
    keys_all = jnp.concatenate([rot_k, norm_tk], axis=0)
    values_all = jnp.concatenate([video_v, text_v], axis=0).reshape(TOKENS + TXT, HEADS, HD)
    valid = jnp.concatenate([jnp.ones((TOKENS,), jnp.int32), text_mask.astype(jnp.int32)]) > 0

    def one_head(triple):
        return attend_head(triple[0], triple[1], triple[2], valid)
    joint = lax.map(one_head, (queries.transpose(1, 0, 2), keys_all.transpose(1, 0, 2), values_all.transpose(1, 0, 2)))
    joint = joint.transpose(1, 0, 2).reshape(TOKENS + TXT, D)
    return (joint[:TOKENS], joint[TOKENS:])
```

```python
import functools
import math

import jax
import jax.numpy as jnp
import numpy as np
from jax import lax
from jax.experimental import pallas as pl
from jax.experimental.pallas import tpu as pltpu
from jax.sharding import Mesh
from jax.sharding import PartitionSpec as P

HD = 128
RT = 16
RH = 56
RW = 56
HEADS = 24
GROUPS = 8
PER = HEADS // GROUPS
TOK = 64
TT = 4
KVROWS = 2 * PER * TOK + 32
QROWS = PER * TOK + 16
QT = GROUPS * TOK + 16
OT = QT + 16
BACK = PER * TOK + PER * 16
SCALE = math.log2(math.e) / math.sqrt(HD)
NT = (((1,), (1,)), ((), ()))
Z = ("zh", "zl")
ALL = ("zl", "y", "x", "zh", "c")
VMEM = 56 * 2**20
F32 = jnp.float32
BF16 = jnp.bfloat16


def lane_tables():
    freqs, part = [], []
    for number, width in enumerate((RT, RH, RW)):
        index = np.arange(width // 2, dtype=np.float32)
        freqs.append(np.power(np.float32(256.0), (-2.0 * index / width).astype(np.float32)))
        part.append(np.full((width // 2,), number))
    freqs = np.repeat(np.concatenate(freqs), 2).astype(np.float32)
    part = np.repeat(np.concatenate(part), 2)
    return freqs, part


def rotary_tables(frames, rows_pos, cols_pos):
    freqs, part = lane_tables()
    position = jnp.where(
        part[None, :] == 0,
        frames[:, None],
        jnp.where(part[None, :] == 1, rows_pos[:, None], cols_pos[:, None]),
    )
    angle = position.astype(F32) * freqs[None, :]
    sign = np.where(np.arange(HD) % 2 == 0, -1.0, 1.0).astype(np.float32)
    return jnp.cos(angle), jnp.sin(angle) * sign[None, :]


def norm(values, gain):
    values = values.astype(F32)
    meansq = jnp.mean(values * values, axis=-1, keepdims=True)
    return values * lax.rsqrt(meansq + 1e-06) * gain


def prep_kernel(place, q, k, v, tq, tk, tv, mask, qg, kg, tqg, tkg, cosine, sine, kv_out, q_out):
    even = lax.broadcasted_iota(jnp.int32, (TOK, HD), 1) % 2 == 0
    cos, sin = cosine[...], sine[...]

    def turn(values, gain):
        x = norm(values, gain)
        swapped = jnp.where(even, pltpu.roll(x, HD - 1, 1), pltpu.roll(x, 1, 1))
        return (x * cos + swapped * sin).astype(BF16)

    for head in range(HEADS):
        group, h = divmod(head, PER)
        lanes = slice(head * HD, (head + 1) * HD)
        q_out[group, h * TOK : (h + 1) * TOK, :] = turn(q[:, lanes], qg[...])
        kv_out[group, h * TOK : (h + 1) * TOK, :] = turn(k[:, lanes], kg[...])
        kv_out[group, (PER + h) * TOK : (PER + h + 1) * TOK, :] = v[:, lanes]
    own = place[0]
    zero4 = jnp.zeros((TT, HD), F32)
    tqs, tks, tvs = tq[...].astype(F32), tk[...].astype(F32), tv[...].astype(F32)
    for pair in range(2):
        qrows, krows = [], []
        for h in range(PER):
            at = (pair * PER + h) * HD
            lanes = slice(at, at + HD)
            qrows.append(norm(tqs[:, lanes], tqg[...]))
            krows.append(norm(tks[:, lanes], tkg[...]))
            krows.append(tvs[:, lanes])
        qrows = jnp.concatenate(qrows + [zero4], axis=0)
        krows = jnp.concatenate(krows + [mask[...].astype(F32), zero4], axis=0)
        for group in range(pair, GROUPS, 2):
            mine = own == group // 2
            q_out[group, PER * TOK :, :] = jnp.where(mine, qrows, 0.0).astype(BF16)
            kv_out[group, 2 * PER * TOK :, :] = jnp.where(mine, krows, 0.0).astype(BF16)


def attend_kernel(q, qtext, k, v, text, out, qs, *, block):
    h = pl.program_id(0)
    qs[: GROUPS * TOK, :] = q[...].reshape(GROUPS * TOK, HD)
    rows = qtext[...].astype(F32)
    rows = rows[:4] + rows[4:]
    top = rows[:, :8]
    upper = lax.broadcasted_iota(jnp.int32, (2, 8, HD), 1) < TT

    def pairs(tile, low):
        tile = tile.reshape(2, 2, 8, HD)
        first, second = tile[:, 0], tile[:, 1]
        if low:
            return jnp.where(upper, first, pltpu.roll(second, TT, 1)).reshape(16, HD)
        return jnp.where(upper, pltpu.roll(first, TT, 1), second).reshape(16, HD)

    chosen = jnp.where(h == 0, pairs(top, True), jnp.where(h == 1, pairs(top, False), pairs(rows[:, 8:], True)))
    qs[GROUPS * TOK :, :] = chosen.astype(BF16)
    queries = qs[...]

    both = text[...].astype(F32).reshape(4, 2, 2, 4, 32, HD)
    both = (both[:, 0, 0] + both[:, 0, 1] + both[:, 1, 0] + both[:, 1, 1]).reshape(16, 32, HD)
    tile = jnp.where(h == 0, both[:, :8], jnp.where(h == 1, both[:, 8:16], both[:, 16:24]))
    tkeys = tile.reshape(HD, HD).astype(BF16)
    tvalues = pltpu.roll(tile, TT, 1).reshape(HD, HD).astype(BF16)
    valid = both[:, 24:32].reshape(HD, HD).T[:1, :] > 0.0

    scores = lax.dot_general(queries, tkeys, NT, preferred_element_type=F32) * SCALE
    scores = jnp.where(valid, scores, -1e30)
    largest = jnp.max(scores, axis=1, keepdims=True)
    weights = jnp.where(valid, jnp.exp2(scores - largest), 0.0).astype(BF16)
    ones = jnp.ones((HD, HD), BF16)
    accum = jnp.dot(weights, jnp.concatenate([tvalues, ones], axis=1), preferred_element_type=F32)
    ones = jnp.ones((block, HD), BF16)
    step = block // TOK
    for at in range(0, k.shape[0], step):
        keys = k[at : at + step].reshape(block, HD)
        values = v[at : at + step].reshape(block, HD)
        scores = lax.dot_general(queries, keys, NT, preferred_element_type=F32) * SCALE
        newest = jnp.maximum(largest, jnp.max(scores, axis=1, keepdims=True))
        weights = jnp.exp2(scores - newest).astype(BF16)
        mixed = jnp.dot(weights, jnp.concatenate([values, ones], axis=1), preferred_element_type=F32)
        accum = accum * jnp.exp2(largest - newest) + mixed
        largest = newest
    total = accum[:, HD:]
    out[0, :QT, :] = (accum[:, :HD] / total).astype(BF16)
    logs = largest + jnp.log2(total)
    logs = jnp.concatenate([logs, jnp.zeros((5 * HD - QT, HD), F32)], axis=0).T[:1, :]
    logs = jnp.concatenate([logs[:, i * HD : (i + 1) * HD] for i in range(5)], axis=0)
    high = logs.astype(BF16).astype(F32)
    middle = (logs - high).astype(BF16).astype(F32)
    low = logs - high - middle
    out[0, QT:, :] = jnp.concatenate([high, middle, low, jnp.zeros((1, HD), F32)], axis=0).astype(BF16)


def combine_kernel(parts, out):
    logs = []
    for s in range(4):
        pieces = parts[s, 0, QT:, :].astype(F32)
        logs.append(pieces[0:5] + pieces[5:10] + pieces[10:15])
    top = functools.reduce(jnp.maximum, logs)
    shares = [jnp.exp2(l - top) for l in logs]
    total = sum(shares)
    shares = [s / total for s in shares]

    def spread(share):
        row = jnp.concatenate([share[i : i + 1] for i in range(5)], axis=1)
        return jnp.broadcast_to(row, (HD, 5 * HD)).T[:QT]

    mixed = sum(spread(shares[s]) * parts[s, 0, :QT, :].astype(F32) for s in range(4)).astype(BF16)
    h = pl.program_id(0)
    video = mixed[: GROUPS * TOK].reshape(GROUPS, TOK, HD)
    text = jnp.broadcast_to(mixed[GROUPS * TOK :][None], (GROUPS, 16, HD))
    for i in range(PER):

        @pl.when(h == i)
        def _():
            out[:, i * TOK : (i + 1) * TOK, :] = video
            out[:, PER * TOK + i * 16 : PER * TOK + (i + 1) * 16, :] = text


def final_kernel(place, parts, video, text):
    for head in range(HEADS):
        group, h = divmod(head, PER)
        video[:, head * HD : (head + 1) * HD] = parts[group, h * TOK : (h + 1) * TOK, :]
    own, zl = place[0], place[1]
    rows = lax.broadcasted_iota(jnp.int32, (8, 16), 0)
    columns = lax.broadcasted_iota(jnp.int32, (8, 16), 1)
    pick = (columns == rows + TT * zl).astype(F32).astype(BF16)
    for pair in range(2):
        for h in range(PER):
            at = PER * TOK + h * 16
            piece = jnp.zeros((16, HD), F32)
            for u in range(4):
                piece += jnp.where(own == u, parts[2 * u + pair, at : at + 16, :].astype(F32), 0.0)
            chosen = jnp.dot(pick, piece.astype(BF16), preferred_element_type=F32)
            lanes = (pair * PER + h) * HD
            text[:, lanes : lanes + HD] = chosen[:TT].astype(BF16)


def whole(*shapes):
    return [pl.BlockSpec(memory_space=pltpu.VMEM) for _ in shapes]


def body(
    video_q,
    video_k,
    video_v,
    text_q,
    text_k,
    text_v,
    video_q_gain,
    video_k_gain,
    text_q_gain,
    text_k_gain,
    frame_ids,
    row_ids,
    col_ids,
    text_mask,
):
    own = 2 * lax.axis_index("zh") + lax.axis_index("c")
    place = jnp.stack([own, lax.axis_index("zl")]).astype(jnp.int32)
    params = pltpu.CompilerParams(vmem_limit_bytes=VMEM)
    cosine, sine = rotary_tables(frame_ids, row_ids, col_ids)
    mask = jnp.broadcast_to(text_mask[:, None], (TT, HD))
    gains = [g.reshape(1, HD) for g in (video_q_gain, video_k_gain, text_q_gain, text_k_gain)]
    operands = (video_q, video_k, video_v, text_q, text_k, text_v, mask, *gains, cosine, sine)
    kv, q = pl.pallas_call(
        prep_kernel,
        out_shape=(
            jax.ShapeDtypeStruct((GROUPS, KVROWS, HD), BF16),
            jax.ShapeDtypeStruct((GROUPS, QROWS, HD), BF16),
        ),
        in_specs=[pl.BlockSpec(memory_space=pltpu.SMEM)] + whole(*operands),
        out_specs=tuple(whole(0, 0)),
        compiler_params=params,
        name="prep",
    )(place, *operands)
    kv = lax.all_to_all(kv, Z, split_axis=0, concat_axis=0, tiled=True)
    q = lax.all_to_all(q, Z, split_axis=0, concat_axis=0, tiled=True)
    kv = lax.all_gather(kv, ("y", "c"), axis=0, tiled=True)
    q = lax.all_gather(q, "x", axis=0, tiled=True)
    sources = kv.shape[0]
    parts = pl.pallas_call(
        functools.partial(attend_kernel, block=1024),
        grid=(PER, 4),
        in_specs=[
            pl.BlockSpec((GROUPS, TOK, HD), lambda h, x: (x, h, 0)),
            pl.BlockSpec((GROUPS, 16, HD), lambda h, x: (x, PER * TOK // 16, 0)),
            pl.BlockSpec((sources, TOK, HD), lambda h, x: (0, h, 0)),
            pl.BlockSpec((sources, TOK, HD), lambda h, x: (0, PER + h, 0)),
            pl.BlockSpec((sources, 32, HD), lambda h, x: (0, 2 * PER * TOK // 32, 0)),
        ],
        out_specs=pl.BlockSpec((1, OT, HD), lambda h, x: (x, h, 0)),
        out_shape=jax.ShapeDtypeStruct((4, PER * OT, HD), BF16),
        scratch_shapes=[pltpu.VMEM((QT, HD), BF16)],
        compiler_params=params,
        name="attend",
    )(q, q, kv, kv, kv)
    parts = lax.all_to_all(parts, "x", split_axis=0, concat_axis=0, tiled=True)
    back = pl.pallas_call(
        combine_kernel,
        grid=(PER,),
        in_specs=[pl.BlockSpec((4, 1, OT, HD), lambda h: (0, h, 0, 0))],
        out_specs=pl.BlockSpec((GROUPS, BACK, HD), lambda h: (0, 0, 0)),
        out_shape=jax.ShapeDtypeStruct((GROUPS, BACK, HD), BF16),
        compiler_params=params,
        name="combine",
    )(parts.reshape(4, PER, OT, HD))
    back = lax.all_to_all(back, Z, split_axis=0, concat_axis=0, tiled=True)
    return pl.pallas_call(
        final_kernel,
        out_shape=(
            jax.ShapeDtypeStruct(video_q.shape, BF16),
            jax.ShapeDtypeStruct(text_q.shape, BF16),
        ),
        in_specs=[pl.BlockSpec(memory_space=pltpu.SMEM)] + whole(0),
        out_specs=tuple(whole(0, 0)),
        compiler_params=params,
        name="final",
    )(place, back)


def solution(mesh):
    devices = mesh.devices.reshape(4, 4, 4, 2, 2)
    mesh = Mesh(devices, ALL)
    tokens = P(ALL, None)
    text = P(("zl", "y", "x"), ("zh", "c"))
    ids = P(ALL)
    in_specs = (tokens, tokens, tokens, text, text, text, P(), P(), P(), P(), ids, ids, ids, P(("zl", "y", "x")))
    out_specs = (tokens, text)
    return jax.shard_map(body, mesh=mesh, in_specs=in_specs, out_specs=out_specs, check_vma=False)
```

```python
import functools
import math

import jax
import jax.numpy as jnp
import numpy as np
from jax import lax
from jax.experimental import pallas as pl
from jax.experimental.pallas import tpu as pltpu
from jax.sharding import Mesh
from jax.sharding import PartitionSpec as P

HD = 128
RT = 16
RH = 56
RW = 56
HEADS = 24
GROUPS = 8
PER = HEADS // GROUPS
TOK = 64
TT = 4
KVROWS = 2 * PER * TOK + 32
QROWS = PER * TOK + 16
QT = GROUPS * TOK + 16
OT = QT + 16
BACK = PER * TOK + 16
LIMIT = 100.0
SCALE = math.log2(math.e) / math.sqrt(HD)
NT = (((1,), (1,)), ((), ()))
Z = ("zh", "zl")
ALL = ("zl", "y", "x", "zh", "c")
VMEM = 56 * 2**20
F32 = jnp.float32
BF16 = jnp.bfloat16


def lane_tables():
    freqs, part = [], []
    for number, width in enumerate((RT, RH, RW)):
        index = np.arange(width // 2, dtype=np.float32)
        freqs.append(np.power(np.float32(256.0), (-2.0 * index / width).astype(np.float32)))
        part.append(np.full((width // 2,), number))
    freqs = np.repeat(np.concatenate(freqs), 2).astype(np.float32)
    part = np.repeat(np.concatenate(part), 2)
    return freqs, part


def norm(values, gain):
    values = values.astype(F32)
    meansq = jnp.mean(values * values, axis=-1, keepdims=True)
    return values * lax.rsqrt(meansq + 1e-06) * gain


def own_group():
    return 2 * lax.axis_index("zh") + lax.axis_index("c")


def turn(values, gain, cos, sin):
    even = lax.broadcasted_iota(jnp.int32, (TOK, HD), 1) % 2 == 0
    x = norm(values, gain)
    swapped = jnp.where(even, pltpu.roll(x, HD - 1, 1), pltpu.roll(x, 1, 1))
    return (x * cos + swapped * sin).astype(BF16)


def prep_kv_kernel(mask, k, v, tk, tv, kg, tkg, frames, rows, cols, freqs, part, kv_out, tables):
    spots = jnp.concatenate([frames[...], rows[...], cols[...], jnp.zeros((5, TOK), jnp.int32)], axis=0)
    position = lax.dot_general(
        spots.astype(F32).astype(BF16), part[...], (((0,), (0,)), ((), ())), preferred_element_type=F32
    )
    angle = position * freqs[...]
    lane = lax.broadcasted_iota(jnp.int32, (TOK, HD), 1)
    cos = jnp.cos(angle)
    sin = jnp.sin(angle)
    sin = jnp.where(lane % 2 == 0, -sin, sin)
    tables[0] = cos
    tables[1] = sin
    for head in range(HEADS):
        group, h = divmod(head, PER)
        lanes = slice(head * HD, (head + 1) * HD)
        kv_out[group, h * TOK : (h + 1) * TOK, :] = turn(k[:, lanes], kg[...], cos, sin)
        kv_out[group, (PER + h) * TOK : (PER + h + 1) * TOK, :] = v[:, lanes]
    own = own_group()
    tks, tvs = tk[...].astype(F32), tv[...].astype(F32)
    token = lax.broadcasted_iota(jnp.int32, (2 * TT, HD), 0)
    last = jnp.zeros((2 * TT, HD), F32)
    for t in range(TT):
        last = jnp.where(token == t, mask[t].astype(F32), last)
    for pair in range(2):
        krows = []
        for h in range(PER):
            lanes = slice((pair * PER + h) * HD, (pair * PER + h + 1) * HD)
            krows.append(norm(tks[:, lanes], tkg[...]))
            krows.append(tvs[:, lanes])
        krows = jnp.concatenate(krows + [last], axis=0)
        for group in range(pair, GROUPS, 2):
            kv_out[group, 2 * PER * TOK :, :] = jnp.where(own == group // 2, krows, 0.0).astype(BF16)


def prep_q_kernel(q, tq, qg, tqg, tables, q_out):
    cos, sin = tables[0], tables[1]
    for head in range(HEADS):
        group, h = divmod(head, PER)
        lanes = slice(head * HD, (head + 1) * HD)
        q_out[group, h * TOK : (h + 1) * TOK, :] = turn(q[:, lanes], qg[...], cos, sin)
    own = own_group()
    tqs = tq[...].astype(F32)
    for pair in range(2):
        qrows = []
        for h in range(PER):
            lanes = slice((pair * PER + h) * HD, (pair * PER + h + 1) * HD)
            qrows.append(norm(tqs[:, lanes], tqg[...]))
        qrows = jnp.concatenate(qrows + [jnp.zeros((TT, HD), F32)], axis=0)
        for group in range(pair, GROUPS, 2):
            q_out[group, PER * TOK :, :] = jnp.where(own == group // 2, qrows, 0.0).astype(BF16)


def attend_kernel(gains, q, qtext, *refs):
    out, qs = refs[-2:]
    count = (len(refs) - 2) // 3
    ks, vs, texts = refs[:count], refs[count : 2 * count], refs[2 * count : 3 * count]
    h = pl.program_id(0)
    qs[: GROUPS * TOK, :] = q[...].reshape(GROUPS * TOK, HD)
    rows = qtext[...].astype(F32)
    rows = rows[:4] + rows[4:]
    top = rows[:, :8]
    upper = lax.broadcasted_iota(jnp.int32, (2, 8, HD), 1) < TT

    def pairs(tile, low):
        tile = tile.reshape(2, 2, 8, HD)
        first, second = tile[:, 0], tile[:, 1]
        if low:
            return jnp.where(upper, first, pltpu.roll(second, TT, 1)).reshape(16, HD)
        return jnp.where(upper, pltpu.roll(first, TT, 1), second).reshape(16, HD)

    chosen = jnp.where(h == 0, pairs(top, True), jnp.where(h == 1, pairs(top, False), pairs(rows[:, 8:], True)))
    qs[GROUPS * TOK :, :] = chosen.astype(BF16)
    queries = qs[...]

    both = []
    for one, other in zip(texts[::2], texts[1::2]):
        tile = one[...].astype(F32) + other[...].astype(F32)
        both.append(tile[:4] + tile[4:])
    both = jnp.concatenate(both, axis=0)
    tile = jnp.where(h == 0, both[:, :8], jnp.where(h == 1, both[:, 8:16], both[:, 16:24]))
    tkeys = tile.reshape(HD, HD).astype(BF16)
    tvalues = pltpu.roll(tile, TT, 1).reshape(HD, HD).astype(BF16)
    valid = both[:, 24:32].reshape(HD, HD).T[:1, :] > 0.0
    block = GROUPS * TOK
    ones = jnp.ones((block, HD), BF16)

    def score(keys):
        return lax.dot_general(queries, keys, NT, preferred_element_type=F32) * SCALE

    def mix(weights, values):
        values = jnp.concatenate([values, ones[: values.shape[0]]], axis=1)
        return jnp.dot(weights.astype(BF16), values, preferred_element_type=F32)

    def finish(accum, logs):
        total = accum[:, HD:]
        out[0, :QT, :] = (accum[:, :HD] / total).astype(BF16)
        logs = logs + jnp.log2(total)
        logs = jnp.concatenate([logs, jnp.zeros((5 * HD - QT, HD), F32)], axis=0).T[:1, :]
        logs = jnp.concatenate([logs[:, i * HD : (i + 1) * HD] for i in range(5)], axis=0)
        high = logs.astype(BF16).astype(F32)
        middle = (logs - high).astype(BF16).astype(F32)
        low = logs - high - middle
        out[0, QT:, :] = jnp.concatenate([high, middle, low, jnp.zeros((1, HD), F32)], axis=0).astype(BF16)

    strongest = jnp.max(jnp.abs(gains[...]), axis=1, keepdims=True)
    reach = jnp.max(strongest[0:2]) * jnp.max(strongest[2:4]) * (HD * SCALE * 1.01)
    bounded = reach <= LIMIT

    @pl.when(bounded)
    def _():
        accum = mix(jnp.where(valid, jnp.exp2(score(tkeys)), 0.0), tvalues)
        for k, v in zip(ks, vs):
            accum += mix(jnp.exp2(score(k[...].reshape(block, HD))), v[...].reshape(block, HD))
        finish(accum, 0.0)

    @pl.when(jnp.logical_not(bounded))
    def _():
        scores = jnp.where(valid, score(tkeys), -1e30)
        largest = jnp.max(scores, axis=1, keepdims=True)
        accum = mix(jnp.where(valid, jnp.exp2(scores - largest), 0.0), tvalues)
        for k, v in zip(ks, vs):
            scores = score(k[...].reshape(block, HD))
            newest = jnp.maximum(largest, jnp.max(scores, axis=1, keepdims=True))
            accum = accum * jnp.exp2(largest - newest) + mix(jnp.exp2(scores - newest), v[...].reshape(block, HD))
            largest = newest
        finish(accum, largest)


def combine_kernel(*refs):
    parts, out = refs[:-1], refs[-1]

    def spread(share):
        row = jnp.concatenate([share[i : i + 1] for i in range(5)], axis=1)
        return jnp.broadcast_to(row, (HD, 5 * HD)).T[:QT]

    texts = []
    for h in range(PER):
        logs = []
        for part in parts:
            pieces = part[h, QT:, :].astype(F32)
            logs.append(pieces[0:5] + pieces[5:10] + pieces[10:15])
        top = functools.reduce(jnp.maximum, logs)
        shares = [jnp.exp2(l - top) for l in logs]
        total = sum(shares)
        mixed = sum(spread(share / total) * part[h, :QT, :].astype(F32) for share, part in zip(shares, parts))
        out[:, h * TOK : (h + 1) * TOK, :] = mixed[: GROUPS * TOK].reshape(GROUPS, TOK, HD).astype(BF16)
        texts.append(mixed[GROUPS * TOK :])
    for zl in range(4):
        rows = [text[zl * TT : (zl + 1) * TT] for text in texts]
        rows = jnp.concatenate(rows + [jnp.zeros((TT, HD), F32)], axis=0).astype(BF16)
        for zh in range(2):
            out[4 * zh + zl, PER * TOK :, :] = rows


def final_kernel(parts, video, text):
    for head in range(HEADS):
        group, h = divmod(head, PER)
        video[:, head * HD : (head + 1) * HD] = parts[group, h * TOK : (h + 1) * TOK, :]
    own = own_group()
    for pair in range(2):
        piece = jnp.zeros((16, HD), F32)
        for u in range(4):
            piece += jnp.where(own == u, parts[2 * u + pair, PER * TOK :, :].astype(F32), 0.0)
        for h in range(PER):
            lanes = (pair * PER + h) * HD
            text[:, lanes : lanes + HD] = piece[h * TT : (h + 1) * TT].astype(BF16)


def shift(values, axis, by):
    n = lax.axis_size(axis)
    return lax.ppermute(values, axis, [(i, (i + by) % n) for i in range(n)])


def whole(*shapes):
    return [pl.BlockSpec(memory_space=pltpu.VMEM) for _ in shapes]


def body(
    video_q,
    video_k,
    video_v,
    text_q,
    text_k,
    text_v,
    video_q_gain,
    video_k_gain,
    text_q_gain,
    text_k_gain,
    frame_ids,
    row_ids,
    col_ids,
    text_mask,
):
    params = pltpu.CompilerParams(vmem_limit_bytes=VMEM)
    gains = [g.reshape(1, HD) for g in (video_q_gain, text_q_gain, video_k_gain, text_k_gain)]
    ids = [i.reshape(1, TOK) for i in (frame_ids, row_ids, col_ids)]
    freqs, part = lane_tables()
    spots = (part[None, :] == np.arange(8)[:, None]).astype(jnp.bfloat16)
    operands = (video_k, video_v, text_k, text_v, gains[2], gains[3], *ids, freqs.reshape(1, HD), spots)
    kv, tables = pl.pallas_call(
        prep_kv_kernel,
        out_shape=(
            jax.ShapeDtypeStruct((GROUPS, KVROWS, HD), BF16),
            jax.ShapeDtypeStruct((2, TOK, HD), F32),
        ),
        in_specs=[pl.BlockSpec(memory_space=pltpu.SMEM)] + whole(*operands),
        out_specs=tuple(whole(0, 0)),
        compiler_params=params,
        name="prep_kv",
    )(text_mask, *operands)
    operands = (video_q, text_q, gains[0], gains[1], tables)
    q = pl.pallas_call(
        prep_q_kernel,
        out_shape=jax.ShapeDtypeStruct((GROUPS, QROWS, HD), BF16),
        in_specs=whole(*operands),
        out_specs=whole(0)[0],
        compiler_params=params,
        name="prep_q",
    )(*operands)
    kv = lax.all_to_all(kv, Z, split_axis=0, concat_axis=0, tiled=True)
    kv, q = lax.optimization_barrier((kv, q))
    held = [kv] + [shift(kv, "y", s) for s in (1, 3, 2)]
    q = lax.all_to_all(q, Z, split_axis=0, concat_axis=0, tiled=True)
    kvs = []
    for mine in held:
        kvs += [mine, shift(mine, "c", 1)]
    tiles = {0: q}
    for s in (3, 1, 2):
        tiles[s] = shift(q, "x", s)
    strength = jnp.concatenate(gains, axis=0)
    attend = pl.pallas_call(
        attend_kernel,
        grid=(PER,),
        in_specs=[
            pl.BlockSpec((4, HD), lambda h: (0, 0)),
            pl.BlockSpec((GROUPS, TOK, HD), lambda h: (0, h, 0)),
            pl.BlockSpec((GROUPS, 16, HD), lambda h: (0, PER * TOK // 16, 0)),
        ]
        + [pl.BlockSpec((GROUPS, TOK, HD), lambda h: (0, h, 0)) for _ in kvs]
        + [pl.BlockSpec((GROUPS, TOK, HD), lambda h: (0, PER + h, 0)) for _ in kvs]
        + [pl.BlockSpec((GROUPS, 32, HD), lambda h: (0, 2 * PER * TOK // 32, 0)) for _ in kvs],
        out_specs=pl.BlockSpec((1, OT, HD), lambda h: (h, 0, 0)),
        out_shape=jax.ShapeDtypeStruct((PER, OT, HD), BF16),
        scratch_shapes=[pltpu.VMEM((QT, HD), BF16)],
        compiler_params=params,
        name="attend",
    )
    parts = []
    for s in (3, 1, 2, 0):
        tile = tiles[s]
        if parts:
            tile, parts[-1] = lax.optimization_barrier((tile, parts[-1]))
        parts.append(attend(strength, tile, tile, *kvs, *kvs, *kvs))
    parts = [shift(p, "x", 4 - s) if s else p for p, s in zip(parts, (3, 1, 2, 0))]
    back = pl.pallas_call(
        combine_kernel,
        out_shape=jax.ShapeDtypeStruct((GROUPS, BACK, HD), BF16),
        in_specs=whole(*parts),
        out_specs=whole(0)[0],
        compiler_params=params,
        name="combine",
    )(*parts)
    back = lax.all_to_all(back, Z, split_axis=0, concat_axis=0, tiled=True)
    return pl.pallas_call(
        final_kernel,
        out_shape=(
            jax.ShapeDtypeStruct(video_q.shape, BF16),
            jax.ShapeDtypeStruct(text_q.shape, BF16),
        ),
        in_specs=whole(0),
        out_specs=tuple(whole(0, 0)),
        compiler_params=params,
        name="final",
    )(back)


def solution(mesh):
    devices = mesh.devices.reshape(4, 4, 4, 2, 2)
    mesh = Mesh(devices, ALL)
    tokens = P(ALL, None)
    text = P(("zl", "y", "x"), ("zh", "c"))
    ids = P(ALL)
    in_specs = (tokens, tokens, tokens, text, text, text, P(), P(), P(), P(), ids, ids, ids, P(("zl", "y", "x")))
    out_specs = (tokens, text)
    return jax.shard_map(body, mesh=mesh, in_specs=in_specs, out_specs=out_specs, check_vma=False)
```

```python
import functools
import math

import jax
import jax.numpy as jnp
import numpy as np
from jax import lax
from jax.experimental import pallas as pl
from jax.experimental.pallas import tpu as pltpu
from jax.sharding import Mesh
from jax.sharding import PartitionSpec as P

HD = 128
RT = 16
RH = 56
RW = 56
HEADS = 24
GROUPS = 8
PER = HEADS // GROUPS
TOK = 64
TT = 4
KVROWS = 2 * PER * TOK + 32
QROWS = PER * TOK + 16
QT = GROUPS * TOK + 16
OT = QT + 16
BACK = PER * TOK + 16
LIMIT = 100.0
SCALE = math.log2(math.e) / math.sqrt(HD)
NT = (((1,), (1,)), ((), ()))
Z = ("zh", "zl")
ALL = ("zl", "y", "x", "zh", "c")
VMEM = 24 * 2**20
F32 = jnp.float32
BF16 = jnp.bfloat16


def lane_tables():
    freqs, part = [], []
    for number, width in enumerate((RT, RH, RW)):
        index = np.arange(width // 2, dtype=np.float32)
        freqs.append(np.power(np.float32(256.0), (-2.0 * index / width).astype(np.float32)))
        part.append(np.full((width // 2,), number))
    freqs = np.repeat(np.concatenate(freqs), 2).astype(np.float32)
    part = np.repeat(np.concatenate(part), 2)
    return freqs, part


def norm(values, gain):
    values = values.astype(F32)
    meansq = jnp.mean(values * values, axis=-1, keepdims=True)
    return values * lax.rsqrt(meansq + 1e-06) * gain


def own_group():
    return 2 * lax.axis_index("zh") + lax.axis_index("c")


def turn(values, gain, cos, sin):
    even = lax.broadcasted_iota(jnp.int32, (TOK, HD), 1) % 2 == 0
    x = norm(values, gain)
    swapped = jnp.where(even, pltpu.roll(x, HD - 1, 1), pltpu.roll(x, 1, 1))
    return (x * cos + swapped * sin).astype(BF16)


def prep_kv_kernel(mask, k, v, tk, tv, kg, tkg, frames, rows, cols, freqs, part, kv_out, tables):
    spots = jnp.concatenate([frames[...], rows[...], cols[...], jnp.zeros((5, TOK), jnp.int32)], axis=0)
    position = lax.dot_general(
        spots.astype(F32).astype(BF16), part[...], (((0,), (0,)), ((), ())), preferred_element_type=F32
    )
    angle = position * freqs[...]
    lane = lax.broadcasted_iota(jnp.int32, (TOK, HD), 1)
    cos = jnp.cos(angle)
    sin = jnp.sin(angle)
    sin = jnp.where(lane % 2 == 0, -sin, sin)
    tables[0] = cos
    tables[1] = sin
    for head in range(HEADS):
        group, h = divmod(head, PER)
        lanes = slice(head * HD, (head + 1) * HD)
        kv_out[group, h * TOK : (h + 1) * TOK, :] = turn(k[:, lanes], kg[...], cos, sin)
        kv_out[group, (PER + h) * TOK : (PER + h + 1) * TOK, :] = v[:, lanes]
    own = own_group()
    tks, tvs = tk[...].astype(F32), tv[...].astype(F32)
    token = lax.broadcasted_iota(jnp.int32, (2 * TT, HD), 0)
    last = jnp.zeros((2 * TT, HD), F32)
    for t in range(TT):
        last = jnp.where(token == t, mask[t].astype(F32), last)
    for pair in range(2):
        krows = []
        for h in range(PER):
            lanes = slice((pair * PER + h) * HD, (pair * PER + h + 1) * HD)
            krows.append(norm(tks[:, lanes], tkg[...]))
            krows.append(tvs[:, lanes])
        krows = jnp.concatenate(krows + [last], axis=0)
        for group in range(pair, GROUPS, 2):
            kv_out[group, 2 * PER * TOK :, :] = jnp.where(own == group // 2, krows, 0.0).astype(BF16)


def prep_q_kernel(q, tq, qg, tqg, tables, q_out):
    cos, sin = tables[0], tables[1]
    for head in range(HEADS):
        group, h = divmod(head, PER)
        lanes = slice(head * HD, (head + 1) * HD)
        q_out[group, h * TOK : (h + 1) * TOK, :] = turn(q[:, lanes], qg[...], cos, sin)
    own = own_group()
    tqs = tq[...].astype(F32)
    for pair in range(2):
        qrows = []
        for h in range(PER):
            lanes = slice((pair * PER + h) * HD, (pair * PER + h + 1) * HD)
            qrows.append(norm(tqs[:, lanes], tqg[...]))
        qrows = jnp.concatenate(qrows + [jnp.zeros((TT, HD), F32)], axis=0)
        for group in range(pair, GROUPS, 2):
            q_out[group, PER * TOK :, :] = jnp.where(own == group // 2, qrows, 0.0).astype(BF16)


def attend_kernel(gains, q, *refs, heads):
    kvs, out = refs[:-1], refs[-1]
    first = heads[0]
    block = GROUPS * TOK
    upper = lax.broadcasted_iota(jnp.int32, (2, 8, HD), 1) < TT

    def pairs(tile, low):
        tile = tile.reshape(2, 2, 8, HD)
        first, second = tile[:, 0], tile[:, 1]
        if low:
            return jnp.where(upper, first, pltpu.roll(second, TT, 1)).reshape(16, HD)
        return jnp.where(upper, pltpu.roll(first, TT, 1), second).reshape(16, HD)

    rows = q[:, PER * TOK :, :].astype(F32)
    rows = rows[:4] + rows[4:]
    qtexts = (pairs(rows[:, :8], True), pairs(rows[:, :8], False), pairs(rows[:, 8:], True))
    both = []
    for one, other in zip(kvs[::2], kvs[1::2]):
        tile = one[:, 2 * PER * TOK :, :].astype(F32) + other[:, 2 * PER * TOK :, :].astype(F32)
        both.append(tile[:4] + tile[4:])
    both = jnp.concatenate(both, axis=0)
    tiles = [both[:, 8 * h : 8 * h + 8] for h in range(PER)]
    valid = both[:, 24:32].reshape(HD, HD).T[:1, :] > 0.0

    strongest = jnp.max(jnp.abs(gains[...]), axis=1, keepdims=True)
    reach = jnp.max(strongest[0:2]) * jnp.max(strongest[2:4]) * (HD * SCALE * 1.01)
    bounded = reach <= LIMIT

    def head(h):
        if isinstance(h, int):
            at, qtext, tile = h * TOK, qtexts[h], tiles[h]
        else:
            at = pl.multiple_of(h * TOK, TOK)
            qtext = jnp.where(h == 0, qtexts[0], jnp.where(h == 1, qtexts[1], qtexts[2]))
            tile = jnp.where(h == 0, tiles[0], jnp.where(h == 1, tiles[1], tiles[2]))
        queries = jnp.concatenate([q[:, pl.ds(at, TOK), :].reshape(block, HD), qtext.astype(BF16)], axis=0)
        tkeys = tile.reshape(HD, HD).astype(BF16)
        tvalues = pltpu.roll(tile, TT, 1).reshape(HD, HD).astype(BF16)

        def score(keys):
            return lax.dot_general(queries, keys, NT, preferred_element_type=F32) * SCALE

        def mix(weights, values):
            values = jnp.concatenate([values, jnp.ones(values.shape, BF16)], axis=1)
            return jnp.dot(weights.astype(BF16), values, preferred_element_type=F32)

        def blocks():
            for kv in kvs:
                keys = kv[:, pl.ds(at, TOK), :].reshape(block, HD)
                yield keys, kv[:, pl.ds(PER * TOK + at, TOK), :].reshape(block, HD)

        def finish(accum, logs):
            total = accum[:, HD:]
            out[h - first, :QT, :] = (accum[:, :HD] / total).astype(BF16)
            logs = logs + jnp.log2(total)
            logs = jnp.concatenate([logs, jnp.zeros((5 * HD - QT, HD), F32)], axis=0).T[:1, :]
            logs = jnp.concatenate([logs[:, i * HD : (i + 1) * HD] for i in range(5)], axis=0)
            high = logs.astype(BF16).astype(F32)
            middle = (logs - high).astype(BF16).astype(F32)
            low = logs - high - middle
            out[h - first, QT:, :] = jnp.concatenate([high, middle, low, jnp.zeros((1, HD), F32)], axis=0).astype(BF16)

        def fast():
            accum = mix(jnp.where(valid, jnp.exp2(score(tkeys)), 0.0), tvalues)
            for keys, values in blocks():
                accum += mix(jnp.exp2(score(keys)), values)
            finish(accum, 0.0)

        def safe():
            scores = jnp.where(valid, score(tkeys), -1e30)
            largest = jnp.max(scores, axis=1, keepdims=True)
            accum = mix(jnp.where(valid, jnp.exp2(scores - largest), 0.0), tvalues)
            for keys, values in blocks():
                scores = score(keys)
                newest = jnp.maximum(largest, jnp.max(scores, axis=1, keepdims=True))
                accum = accum * jnp.exp2(largest - newest) + mix(jnp.exp2(scores - newest), values)
                largest = newest
            finish(accum, largest)

        return fast, safe

    @pl.when(bounded)
    def _():
        for h in heads:
            head(h)[0]()

    @pl.when(jnp.logical_not(bounded))
    def _():
        @pl.loop(first, heads[-1] + 1)
        def _(h):
            head(h)[1]()


def combine_kernel(*refs):
    parts, (early, late, out) = refs[:-3], refs[-3:]

    def spread(share):
        row = jnp.concatenate([share[i : i + 1] for i in range(5)], axis=1)
        return jnp.broadcast_to(row, (HD, 5 * HD)).T[:QT]

    texts = []
    for h in range(PER):
        own = early.at[h] if h < PER - 1 else late.at[0]
        blocks = [part.at[h] for part in parts] + [own]
        logs = []
        for block in blocks:
            pieces = block[QT:, :].astype(F32)
            logs.append(pieces[0:5] + pieces[5:10] + pieces[10:15])
        top = functools.reduce(jnp.maximum, logs)
        shares = [jnp.exp2(l - top) for l in logs]
        total = sum(shares)
        mixed = sum(spread(share / total) * block[:QT, :].astype(F32) for share, block in zip(shares, blocks))
        out[:, h * TOK : (h + 1) * TOK, :] = mixed[: GROUPS * TOK].reshape(GROUPS, TOK, HD).astype(BF16)
        texts.append(mixed[GROUPS * TOK :])
    for zl in range(4):
        rows = [text[zl * TT : (zl + 1) * TT] for text in texts]
        rows = jnp.concatenate(rows + [jnp.zeros((TT, HD), F32)], axis=0).astype(BF16)
        for zh in range(2):
            out[4 * zh + zl, PER * TOK :, :] = rows


def final_kernel(parts, video, text):
    for head in range(HEADS):
        group, h = divmod(head, PER)
        video[:, head * HD : (head + 1) * HD] = parts[group, h * TOK : (h + 1) * TOK, :]
    own = own_group()
    for pair in range(2):
        piece = jnp.zeros((16, HD), F32)
        for u in range(4):
            piece += jnp.where(own == u, parts[2 * u + pair, PER * TOK :, :].astype(F32), 0.0)
        for h in range(PER):
            lanes = (pair * PER + h) * HD
            text[:, lanes : lanes + HD] = piece[h * TT : (h + 1) * TT].astype(BF16)


def shift(values, axis, by):
    n = lax.axis_size(axis)
    return lax.ppermute(values, axis, [(i, (i + by) % n) for i in range(n)])


def onward(near, axis):
    n = lax.axis_size(axis)
    passed = jnp.where(lax.axis_index("c") == 0, near[0], near[1])
    moves = [(2 * i + c, 2 * ((i + (-1 if c else 1)) % n) + c) for i in range(n) for c in range(2)]
    return lax.ppermute(passed, (axis, "c"), moves)


def whole(*shapes):
    return [pl.BlockSpec(memory_space=pltpu.VMEM) for _ in shapes]


def body(
    video_q,
    video_k,
    video_v,
    text_q,
    text_k,
    text_v,
    video_q_gain,
    video_k_gain,
    text_q_gain,
    text_k_gain,
    frame_ids,
    row_ids,
    col_ids,
    text_mask,
):
    params = pltpu.CompilerParams(vmem_limit_bytes=VMEM)
    gains = [g.reshape(1, HD) for g in (video_q_gain, text_q_gain, video_k_gain, text_k_gain)]
    ids = [i.reshape(1, TOK) for i in (frame_ids, row_ids, col_ids)]
    freqs, part = lane_tables()
    spots = (part[None, :] == np.arange(8)[:, None]).astype(jnp.bfloat16)
    operands = (video_k, video_v, text_k, text_v, gains[2], gains[3], *ids, freqs.reshape(1, HD), spots)
    kv, tables = pl.pallas_call(
        prep_kv_kernel,
        out_shape=(
            jax.ShapeDtypeStruct((GROUPS, KVROWS, HD), BF16),
            jax.ShapeDtypeStruct((2, TOK, HD), F32),
        ),
        in_specs=[pl.BlockSpec(memory_space=pltpu.SMEM)] + whole(*operands),
        out_specs=tuple(whole(0, 0)),
        compiler_params=params,
        name="prep_kv",
    )(text_mask, *operands)
    operands = (video_q, text_q, gains[0], gains[1], tables)
    q = pl.pallas_call(
        prep_q_kernel,
        out_shape=jax.ShapeDtypeStruct((GROUPS, QROWS, HD), BF16),
        in_specs=whole(*operands),
        out_specs=whole(0)[0],
        compiler_params=params,
        name="prep_q",
    )(*operands)
    kv = lax.all_to_all(kv, Z, split_axis=0, concat_axis=0, tiled=True)
    kv, q = lax.optimization_barrier((kv, q))
    near = [shift(kv, "y", 1), shift(kv, "y", 3)]
    kvs = [kv, shift(kv, "c", 1)]
    q = lax.all_to_all(q, Z, split_axis=0, concat_axis=0, tiled=True)
    q, *near = lax.optimization_barrier((q, *near))
    far = onward(near, "y")
    tiles = {0: q, 1: shift(q, "x", 1), 3: shift(q, "x", 3)}
    for mine in (*near, far):
        kvs += [mine, shift(mine, "c", 1)]
    tiles[2] = onward([tiles[1], tiles[3]], "x")
    strength = jnp.concatenate(gains, axis=0)

    def attend(tile, heads):
        operands = (strength, tile, *kvs)
        return pl.pallas_call(
            functools.partial(attend_kernel, heads=heads),
            in_specs=whole(*operands),
            out_specs=whole(0)[0],
            out_shape=jax.ShapeDtypeStruct((len(heads), OT, HD), BF16),
            compiler_params=params,
            name="attend",
        )(*operands)

    every = tuple(range(PER))
    from3 = attend(tiles[3], every)
    tile, from3 = lax.optimization_barrier((tiles[2], from3))
    from3 = shift(from3, "x", 1)
    from2 = attend(tile, every)
    tile, from3, from2 = lax.optimization_barrier((tiles[1], from3, from2))
    from2 = shift(from2, "x", 2)
    from1 = attend(tile, every)
    tile, from1 = lax.optimization_barrier((tiles[0], from1))
    from1 = shift(from1, "x", 3)
    early = attend(tile, every[:-1])
    tile, from2, early = lax.optimization_barrier((tile, from2, early))
    late = attend(tile, every[-1:])
    parts = (from3, from2, from1, early, late)
    back = pl.pallas_call(
        combine_kernel,
        out_shape=jax.ShapeDtypeStruct((GROUPS, BACK, HD), BF16),
        in_specs=whole(*parts),
        out_specs=whole(0)[0],
        compiler_params=params,
        name="combine",
    )(*parts)
    back = lax.all_to_all(back, Z, split_axis=0, concat_axis=0, tiled=True)
    return pl.pallas_call(
        final_kernel,
        out_shape=(
            jax.ShapeDtypeStruct(video_q.shape, BF16),
            jax.ShapeDtypeStruct(text_q.shape, BF16),
        ),
        in_specs=whole(0),
        out_specs=tuple(whole(0, 0)),
        compiler_params=params,
        name="final",
    )(back)


def solution(mesh):
    devices = mesh.devices.reshape(4, 4, 4, 2, 2)
    mesh = Mesh(devices, ALL)
    tokens = P(ALL, None)
    text = P(("zl", "y", "x"), ("zh", "c"))
    ids = P(ALL)
    in_specs = (tokens, tokens, tokens, text, text, text, P(), P(), P(), P(), ids, ids, ids, P(("zl", "y", "x")))
    out_specs = (tokens, text)
    return jax.shard_map(body, mesh=mesh, in_specs=in_specs, out_specs=out_specs, check_vma=False)
```

```python
import functools
import math

import jax
import jax.numpy as jnp
import numpy as np
from jax import lax
from jax.experimental import pallas as pl
from jax.experimental.pallas import tpu as pltpu
from jax.sharding import Mesh
from jax.sharding import PartitionSpec as P

HD = 128
RT = 16
RH = 56
RW = 56
HEADS = 24
GROUPS = 8
PER = HEADS // GROUPS
TOK = 64
TT = 4
KVROWS = 2 * PER * TOK + 32
QROWS = PER * TOK + 16
QT = GROUPS * TOK + 16
OT = QT + 16
BACK = PER * TOK + 16
LIMIT = 100.0
SCALE = math.log2(math.e) / math.sqrt(HD)
NT = (((1,), (1,)), ((), ()))
Z = ("zh", "zl")
ALL = ("zl", "y", "x", "zh", "c")
VMEM = 24 * 2**20
F32 = jnp.float32
BF16 = jnp.bfloat16


def lane_tables():
    freqs, part = [], []
    for number, width in enumerate((RT, RH, RW)):
        index = np.arange(width // 2, dtype=np.float32)
        freqs.append(np.power(np.float32(256.0), (-2.0 * index / width).astype(np.float32)))
        part.append(np.full((width // 2,), number))
    freqs = np.repeat(np.concatenate(freqs), 2).astype(np.float32)
    part = np.repeat(np.concatenate(part), 2)
    return freqs, part


def norm(values, gain):
    values = values.astype(F32)
    meansq = jnp.mean(values * values, axis=-1, keepdims=True)
    return values * lax.rsqrt(meansq + 1e-06) * gain


def own_group():
    return 2 * lax.axis_index("zh") + lax.axis_index("c")


def turn(values, gain, cos, sin):
    even = lax.broadcasted_iota(jnp.int32, (TOK, HD), 1) % 2 == 0
    x = norm(values, gain)
    swapped = jnp.where(even, pltpu.roll(x, HD - 1, 1), pltpu.roll(x, 1, 1))
    return (x * cos + swapped * sin).astype(BF16)


def prep_kv_kernel(mask, k, v, tk, tv, kg, tkg, frames, rows, cols, freqs, part, kv_out, tables):
    spots = jnp.concatenate([frames[...], rows[...], cols[...], jnp.zeros((5, TOK), jnp.int32)], axis=0)
    position = lax.dot_general(
        spots.astype(F32).astype(BF16), part[...], (((0,), (0,)), ((), ())), preferred_element_type=F32
    )
    angle = position * freqs[...]
    lane = lax.broadcasted_iota(jnp.int32, (TOK, HD), 1)
    cos = jnp.cos(angle)
    sin = jnp.sin(angle)
    sin = jnp.where(lane % 2 == 0, -sin, sin)
    tables[0] = cos
    tables[1] = sin
    for head in range(HEADS):
        group, h = divmod(head, PER)
        lanes = slice(head * HD, (head + 1) * HD)
        kv_out[group, h * TOK : (h + 1) * TOK, :] = turn(k[:, lanes], kg[...], cos, sin)
        kv_out[group, (PER + h) * TOK : (PER + h + 1) * TOK, :] = v[:, lanes]
    own = own_group()
    tks, tvs = tk[...].astype(F32), tv[...].astype(F32)
    token = lax.broadcasted_iota(jnp.int32, (2 * TT, HD), 0)
    last = jnp.zeros((2 * TT, HD), F32)
    for t in range(TT):
        last = jnp.where(token == t, mask[t].astype(F32), last)
    for pair in range(2):
        krows = []
        for h in range(PER):
            lanes = slice((pair * PER + h) * HD, (pair * PER + h + 1) * HD)
            krows.append(norm(tks[:, lanes], tkg[...]))
            krows.append(tvs[:, lanes])
        krows = jnp.concatenate(krows + [last], axis=0)
        for group in range(pair, GROUPS, 2):
            kv_out[group, 2 * PER * TOK :, :] = jnp.where(own == group // 2, krows, 0.0).astype(BF16)


def prep_q_kernel(q, tq, qg, tqg, tables, q_out):
    cos, sin = tables[0], tables[1]
    for head in range(HEADS):
        group, h = divmod(head, PER)
        lanes = slice(head * HD, (head + 1) * HD)
        q_out[group, h * TOK : (h + 1) * TOK, :] = turn(q[:, lanes], qg[...], cos, sin)
    own = own_group()
    tqs = tq[...].astype(F32)
    for pair in range(2):
        qrows = []
        for h in range(PER):
            lanes = slice((pair * PER + h) * HD, (pair * PER + h + 1) * HD)
            qrows.append(norm(tqs[:, lanes], tqg[...]))
        qrows = jnp.concatenate(qrows + [jnp.zeros((TT, HD), F32)], axis=0)
        for group in range(pair, GROUPS, 2):
            q_out[group, PER * TOK :, :] = jnp.where(own == group // 2, qrows, 0.0).astype(BF16)


def attend_kernel(gains, q, *refs, heads):
    kvs, out = refs[:-1], refs[-1]
    first = heads[0]
    block = GROUPS * TOK
    upper = lax.broadcasted_iota(jnp.int32, (2, 8, HD), 1) < TT

    def pairs(tile, low):
        tile = tile.reshape(2, 2, 8, HD)
        first, second = tile[:, 0], tile[:, 1]
        if low:
            return jnp.where(upper, first, pltpu.roll(second, TT, 1)).reshape(16, HD)
        return jnp.where(upper, pltpu.roll(first, TT, 1), second).reshape(16, HD)

    rows = q[:, PER * TOK :, :].astype(F32)
    rows = rows[:4] + rows[4:]
    qtexts = (pairs(rows[:, :8], True), pairs(rows[:, :8], False), pairs(rows[:, 8:], True))
    both = []
    for one, other in zip(kvs[::2], kvs[1::2]):
        tile = one[:, 2 * PER * TOK :, :].astype(F32) + other[:, 2 * PER * TOK :, :].astype(F32)
        both.append(tile[:4] + tile[4:])
    both = jnp.concatenate(both, axis=0)
    tiles = [both[:, 8 * h : 8 * h + 8] for h in range(PER)]
    valid = both[:, 24:32].reshape(HD, HD).T[:1, :] > 0.0

    strongest = jnp.max(jnp.abs(gains[...]), axis=1, keepdims=True)
    reach = jnp.max(strongest[0:2]) * jnp.max(strongest[2:4]) * (HD * SCALE * 1.01)
    bounded = reach <= LIMIT

    def head(h):
        if isinstance(h, int):
            at, qtext, tile = h * TOK, qtexts[h], tiles[h]
        else:
            at = pl.multiple_of(h * TOK, TOK)
            qtext = jnp.where(h == 0, qtexts[0], jnp.where(h == 1, qtexts[1], qtexts[2]))
            tile = jnp.where(h == 0, tiles[0], jnp.where(h == 1, tiles[1], tiles[2]))
        queries = jnp.concatenate([q[:, pl.ds(at, TOK), :].reshape(block, HD), qtext.astype(BF16)], axis=0)
        tkeys = tile.reshape(HD, HD).astype(BF16)
        tvalues = pltpu.roll(tile, TT, 1).reshape(HD, HD).astype(BF16)

        def score(keys):
            return lax.dot_general(queries, keys, NT, preferred_element_type=F32) * SCALE

        def mix(weights, values):
            values = jnp.concatenate([values, jnp.ones(values.shape, BF16)], axis=1)
            return jnp.dot(weights.astype(BF16), values, preferred_element_type=F32)

        def blocks():
            for kv in kvs:
                keys = kv[:, pl.ds(at, TOK), :].reshape(block, HD)
                yield keys, kv[:, pl.ds(PER * TOK + at, TOK), :].reshape(block, HD)

        def finish(accum, logs):
            total = accum[:, HD:]
            out[h - first, :QT, :] = (accum[:, :HD] / total).astype(BF16)
            logs = logs + jnp.log2(total)
            logs = jnp.concatenate([logs, jnp.zeros((5 * HD - QT, HD), F32)], axis=0).T[:1, :]
            logs = jnp.concatenate([logs[:, i * HD : (i + 1) * HD] for i in range(5)], axis=0)
            high = logs.astype(BF16).astype(F32)
            middle = (logs - high).astype(BF16).astype(F32)
            low = logs - high - middle
            out[h - first, QT:, :] = jnp.concatenate([high, middle, low, jnp.zeros((1, HD), F32)], axis=0).astype(BF16)

        def fast():
            accum = mix(jnp.where(valid, jnp.exp2(score(tkeys)), 0.0), tvalues)
            for keys, values in blocks():
                accum += mix(jnp.exp2(score(keys)), values)
            finish(accum, 0.0)

        def safe():
            scores = jnp.where(valid, score(tkeys), -1e30)
            largest = jnp.max(scores, axis=1, keepdims=True)
            accum = mix(jnp.where(valid, jnp.exp2(scores - largest), 0.0), tvalues)
            for keys, values in blocks():
                scores = score(keys)
                newest = jnp.maximum(largest, jnp.max(scores, axis=1, keepdims=True))
                accum = accum * jnp.exp2(largest - newest) + mix(jnp.exp2(scores - newest), values)
                largest = newest
            finish(accum, largest)

        return fast, safe

    @pl.when(bounded)
    def _():
        for h in heads:
            head(h)[0]()

    @pl.when(jnp.logical_not(bounded))
    def _():
        @pl.loop(first, heads[-1] + 1)
        def _(h):
            head(h)[1]()


def combine_kernel(*refs):
    parts, (early, late, out) = refs[:-3], refs[-3:]

    def spread(share):
        row = jnp.concatenate([share[i : i + 1] for i in range(5)], axis=1)
        return jnp.broadcast_to(row, (HD, 5 * HD)).T[:QT]

    texts = []
    for h in range(PER):
        own = early.at[h] if h < PER - 1 else late.at[0]
        blocks = [part.at[h] for part in parts] + [own]
        logs = []
        for block in blocks:
            pieces = block[QT:, :].astype(F32)
            logs.append(pieces[0:5] + pieces[5:10] + pieces[10:15])
        top = functools.reduce(jnp.maximum, logs)
        shares = [jnp.exp2(l - top) for l in logs]
        total = sum(shares)
        mixed = sum(spread(share / total) * block[:QT, :].astype(F32) for share, block in zip(shares, blocks))
        out[:, h * TOK : (h + 1) * TOK, :] = mixed[: GROUPS * TOK].reshape(GROUPS, TOK, HD).astype(BF16)
        texts.append(mixed[GROUPS * TOK :])
    for zl in range(4):
        rows = [text[zl * TT : (zl + 1) * TT] for text in texts]
        rows = jnp.concatenate(rows + [jnp.zeros((TT, HD), F32)], axis=0).astype(BF16)
        for zh in range(2):
            out[4 * zh + zl, PER * TOK :, :] = rows


def final_kernel(parts, video, text):
    for head in range(HEADS):
        group, h = divmod(head, PER)
        video[:, head * HD : (head + 1) * HD] = parts[group, h * TOK : (h + 1) * TOK, :]
    own = own_group()
    for pair in range(2):
        piece = jnp.zeros((16, HD), F32)
        for u in range(4):
            piece += jnp.where(own == u, parts[2 * u + pair, PER * TOK :, :].astype(F32), 0.0)
        for h in range(PER):
            lanes = (pair * PER + h) * HD
            text[:, lanes : lanes + HD] = piece[h * TT : (h + 1) * TT].astype(BF16)


def shift(values, axis, by):
    n = lax.axis_size(axis)
    return lax.ppermute(values, axis, [(i, (i + by) % n) for i in range(n)])


def onward(near, axis):
    n = lax.axis_size(axis)
    passed = jnp.where(lax.axis_index("c") == 0, near[0], near[1])
    moves = [(2 * i + c, 2 * ((i + (-1 if c else 1)) % n) + c) for i in range(n) for c in range(2)]
    return lax.ppermute(passed, (axis, "c"), moves)


def whole(*shapes):
    return [pl.BlockSpec(memory_space=pltpu.VMEM) for _ in shapes]


def body(
    video_q,
    video_k,
    video_v,
    text_q,
    text_k,
    text_v,
    video_q_gain,
    video_k_gain,
    text_q_gain,
    text_k_gain,
    frame_ids,
    row_ids,
    col_ids,
    text_mask,
):
    params = pltpu.CompilerParams(vmem_limit_bytes=VMEM)
    alone = pltpu.CompilerParams(vmem_limit_bytes=56 * 2**20)
    gains = [g.reshape(1, HD) for g in (video_q_gain, text_q_gain, video_k_gain, text_k_gain)]
    ids = [i.reshape(1, TOK) for i in (frame_ids, row_ids, col_ids)]
    freqs, part = lane_tables()
    spots = (part[None, :] == np.arange(8)[:, None]).astype(jnp.bfloat16)
    operands = (video_k, video_v, text_k, text_v, gains[2], gains[3], *ids, freqs.reshape(1, HD), spots)
    kv, tables = pl.pallas_call(
        prep_kv_kernel,
        out_shape=(
            jax.ShapeDtypeStruct((GROUPS, KVROWS, HD), BF16),
            jax.ShapeDtypeStruct((2, TOK, HD), F32),
        ),
        in_specs=[pl.BlockSpec(memory_space=pltpu.SMEM)] + whole(*operands),
        out_specs=tuple(whole(0, 0)),
        compiler_params=alone,
        name="prep_kv",
    )(text_mask, *operands)
    operands = (video_q, text_q, gains[0], gains[1], tables)
    q = pl.pallas_call(
        prep_q_kernel,
        out_shape=jax.ShapeDtypeStruct((GROUPS, QROWS, HD), BF16),
        in_specs=whole(*operands),
        out_specs=whole(0)[0],
        compiler_params=alone,
        name="prep_q",
    )(*operands)
    kv = lax.all_to_all(kv, Z, split_axis=0, concat_axis=0, tiled=True)
    kv, q = lax.optimization_barrier((kv, q))
    near = [shift(kv, "y", 1), shift(kv, "y", 3)]
    kvs = [kv, shift(kv, "c", 1)]
    q = lax.all_to_all(q, Z, split_axis=0, concat_axis=0, tiled=True)
    q, *near = lax.optimization_barrier((q, *near))
    far = onward(near, "y")
    tiles = {0: q, 1: shift(q, "x", 1), 3: shift(q, "x", 3)}
    for mine in (*near, far):
        kvs += [mine, shift(mine, "c", 1)]
    tiles[2] = onward([tiles[1], tiles[3]], "x")
    strength = jnp.concatenate(gains, axis=0)

    def attend(tile, heads):
        operands = (strength, tile, *kvs)
        return pl.pallas_call(
            functools.partial(attend_kernel, heads=heads),
            in_specs=whole(*operands),
            out_specs=whole(0)[0],
            out_shape=jax.ShapeDtypeStruct((len(heads), OT, HD), BF16),
            compiler_params=params,
            name="attend",
        )(*operands)

    every = tuple(range(PER))
    from3 = attend(tiles[3], every)
    tile, from3 = lax.optimization_barrier((tiles[2], from3))
    from3 = shift(from3, "x", 1)
    from2 = attend(tile, every)
    tile, from3, from2 = lax.optimization_barrier((tiles[1], from3, from2))
    from2 = shift(from2, "x", 2)
    from1 = attend(tile, every)
    tile, from1 = lax.optimization_barrier((tiles[0], from1))
    from1 = shift(from1, "x", 3)
    early = attend(tile, every[:-1])
    tile, from2, early = lax.optimization_barrier((tile, from2, early))
    late = attend(tile, every[-1:])
    parts = (from3, from2, from1, early, late)
    back = pl.pallas_call(
        combine_kernel,
        out_shape=jax.ShapeDtypeStruct((GROUPS, BACK, HD), BF16),
        in_specs=whole(*parts),
        out_specs=whole(0)[0],
        compiler_params=params,
        name="combine",
    )(*parts)
    back = lax.all_to_all(back, Z, split_axis=0, concat_axis=0, tiled=True)
    return pl.pallas_call(
        final_kernel,
        out_shape=(
            jax.ShapeDtypeStruct(video_q.shape, BF16),
            jax.ShapeDtypeStruct(text_q.shape, BF16),
        ),
        in_specs=whole(0),
        out_specs=tuple(whole(0, 0)),
        compiler_params=params,
        name="final",
    )(back)


def solution(mesh):
    devices = mesh.devices.reshape(4, 4, 4, 2, 2)
    mesh = Mesh(devices, ALL)
    tokens = P(ALL, None)
    text = P(("zl", "y", "x"), ("zh", "c"))
    ids = P(ALL)
    in_specs = (tokens, tokens, tokens, text, text, text, P(), P(), P(), P(), ids, ids, ids, P(("zl", "y", "x")))
    out_specs = (tokens, text)
    return jax.shard_map(body, mesh=mesh, in_specs=in_specs, out_specs=out_specs, check_vma=False)
```

```python
import functools
import math

import jax
import jax.numpy as jnp
import numpy as np
from jax import lax
from jax.experimental import pallas as pl
from jax.experimental.pallas import tpu as pltpu
from jax.sharding import Mesh
from jax.sharding import PartitionSpec as P

HD = 128
RT = 16
RH = 56
RW = 56
HEADS = 24
GROUPS = 8
PER = HEADS // GROUPS
TOK = 64
TT = 4
KVROWS = 2 * PER * TOK + 32
QROWS = PER * TOK + 16
QT = GROUPS * TOK + 16
OT = QT + 16
BACK = PER * TOK + 16
LIMIT = 100.0
SCALE = math.log2(math.e) / math.sqrt(HD)
NT = (((1,), (1,)), ((), ()))
Z = ("zh", "zl")
ALL = ("zl", "y", "x", "zh", "c")
VMEM = 24 * 2**20
F32 = jnp.float32
BF16 = jnp.bfloat16


def lane_tables():
    freqs, part = [], []
    for number, width in enumerate((RT, RH, RW)):
        index = np.arange(width // 2, dtype=np.float32)
        freqs.append(np.power(np.float32(256.0), (-2.0 * index / width).astype(np.float32)))
        part.append(np.full((width // 2,), number))
    freqs = np.repeat(np.concatenate(freqs), 2).astype(np.float32)
    part = np.repeat(np.concatenate(part), 2)
    return freqs, part


def norm(values, gain):
    values = values.astype(F32)
    meansq = jnp.mean(values * values, axis=-1, keepdims=True)
    return values * lax.rsqrt(meansq + 1e-06) * gain


def own_group():
    return 2 * lax.axis_index("zh") + lax.axis_index("c")


def swap_pairs(lanes):
    row = lax.broadcasted_iota(jnp.int32, (lanes, lanes), 0)
    column = lax.broadcasted_iota(jnp.int32, (lanes, lanes), 1)
    return (row == column + 1 - 2 * (column % 2)).astype(F32).astype(BF16)


def turning(gain, cos, sin):
    swap = swap_pairs(HD)
    even = lax.broadcasted_iota(jnp.int32, (8, HD), 1) % 2 == 0
    wide = jnp.broadcast_to(gain, (8, HD))
    other = jnp.where(even, pltpu.roll(wide, HD - 1, 1), pltpu.roll(wide, 1, 1))[:1]
    cos, sin = cos * gain, sin * other

    def turn(values):
        swapped = jnp.dot(values, swap, preferred_element_type=F32)
        x = values.astype(F32)
        scale = lax.rsqrt(jnp.mean(x * x, axis=-1, keepdims=True) + 1e-06)
        return ((x * cos + swapped * sin) * scale).astype(BF16)

    return turn


def prep_kv_kernel(mask, k, v, tk, tv, kg, tkg, frames, rows, cols, freqs, part, kv_out, tables):
    spots = jnp.concatenate([frames[...], rows[...], cols[...], jnp.zeros((5, TOK), jnp.int32)], axis=0)
    position = lax.dot_general(
        spots.astype(F32).astype(BF16), part[...], (((0,), (0,)), ((), ())), preferred_element_type=F32
    )
    angle = position * freqs[...]
    lane = lax.broadcasted_iota(jnp.int32, (TOK, HD), 1)
    cos = jnp.cos(angle)
    sin = jnp.sin(angle)
    sin = jnp.where(lane % 2 == 0, -sin, sin)
    tables[0] = cos
    tables[1] = sin
    turn = turning(kg[...], cos, sin)
    for head in range(HEADS):
        group, h = divmod(head, PER)
        lanes = slice(head * HD, (head + 1) * HD)
        kv_out[group, h * TOK : (h + 1) * TOK, :] = turn(k[:, lanes])
        kv_out[group, (PER + h) * TOK : (PER + h + 1) * TOK, :] = v[:, lanes]
    own = own_group()
    tks, tvs = tk[...].astype(F32), tv[...].astype(F32)
    token = lax.broadcasted_iota(jnp.int32, (2 * TT, HD), 0)
    last = jnp.zeros((2 * TT, HD), F32)
    for t in range(TT):
        last = jnp.where(token == t, mask[t].astype(F32), last)
    for pair in range(2):
        krows = []
        for h in range(PER):
            lanes = slice((pair * PER + h) * HD, (pair * PER + h + 1) * HD)
            krows.append(norm(tks[:, lanes], tkg[...]))
            krows.append(tvs[:, lanes])
        krows = jnp.concatenate(krows + [last], axis=0)
        for group in range(pair, GROUPS, 2):
            kv_out[group, 2 * PER * TOK :, :] = jnp.where(own == group // 2, krows, 0.0).astype(BF16)


def prep_q_kernel(q, tq, qg, tqg, tables, q_out):
    turn = turning(qg[...], tables[0], tables[1])
    for head in range(HEADS):
        group, h = divmod(head, PER)
        lanes = slice(head * HD, (head + 1) * HD)
        q_out[group, h * TOK : (h + 1) * TOK, :] = turn(q[:, lanes])
    own = own_group()
    tqs = tq[...].astype(F32)
    for pair in range(2):
        qrows = []
        for h in range(PER):
            lanes = slice((pair * PER + h) * HD, (pair * PER + h + 1) * HD)
            qrows.append(norm(tqs[:, lanes], tqg[...]))
        qrows = jnp.concatenate(qrows + [jnp.zeros((TT, HD), F32)], axis=0)
        for group in range(pair, GROUPS, 2):
            q_out[group, PER * TOK :, :] = jnp.where(own == group // 2, qrows, 0.0).astype(BF16)


def text_queries(tile):
    upper = lax.broadcasted_iota(jnp.int32, (2, 8, HD), 1) < TT

    def pairs(rows, low):
        rows = rows.reshape(2, 2, 8, HD)
        one, other = rows[:, 0], rows[:, 1]
        if low:
            return jnp.where(upper, one, pltpu.roll(other, TT, 1)).reshape(16, HD)
        return jnp.where(upper, pltpu.roll(one, TT, 1), other).reshape(16, HD)

    rows = tile[:, PER * TOK :, :].astype(F32)
    rows = rows[:4] + rows[4:]
    return pairs(rows[:, :8], True), pairs(rows[:, :8], False), pairs(rows[:, 8:], True)


def split(logs):
    high = logs.astype(BF16).astype(F32)
    middle = (logs - high).astype(BF16).astype(F32)
    return high, middle, logs - high - middle


def attend_kernel(gains, *refs, tiles, ready, heads):
    queries_in, refs = refs[:tiles], refs[tiles:]
    if ready:
        done, refs = refs[0], refs[1:]
    if tiles > 1:
        refs, texts_out = refs[: 1 - tiles], refs[1 - tiles :]
    kvs, out = refs[:-1], refs[-1]
    first = heads[0]
    block = GROUPS * TOK
    texts = [text_queries(q) for q in queries_in] if tiles > 1 else []
    empty = jnp.zeros((1, HD), F32)

    both = []
    for one, other in zip(kvs[::2], kvs[1::2]):
        tile = one[:, 2 * PER * TOK :, :].astype(F32) + other[:, 2 * PER * TOK :, :].astype(F32)
        both.append(tile[:4] + tile[4:])
    both = jnp.concatenate(both, axis=0)
    ttiles = [both[:, 8 * h : 8 * h + 8] for h in range(PER)]
    valid = both[:, 24:32].reshape(HD, HD)[:, :1] > 0.0

    strongest = jnp.max(jnp.abs(gains[...]), axis=1, keepdims=True)
    reach = jnp.max(strongest[0:2]) * jnp.max(strongest[2:4]) * (HD * SCALE * 1.01)
    bounded = reach <= LIMIT

    def head(h, fast):
        at = h * TOK if isinstance(h, int) else pl.multiple_of(h * TOK, TOK)

        def pick(three):
            if isinstance(h, int):
                return three[h]
            return jnp.where(h == 0, three[0], jnp.where(h == 1, three[1], three[2]))

        queries = queries_in[0][:, pl.ds(at, TOK), :].reshape(block, HD)
        if texts:
            rows = [pick(text) for text in texts] + [jnp.zeros((HD - 16 * tiles, HD), F32)]
            queries = jnp.concatenate([queries, jnp.concatenate(rows, axis=0).astype(BF16)], axis=0)
        count = queries.shape[0]

        def absorb(state, keys, values, valid):
            accum, largest = state
            scores = lax.dot_general(keys, queries, NT, preferred_element_type=F32) * SCALE
            values = jnp.concatenate([values.astype(F32).T.astype(BF16), jnp.ones((16, values.shape[0]), BF16)], axis=0)
            if not fast:
                if valid is not None:
                    scores = jnp.where(valid, scores, -1e30)
                newest = jnp.maximum(largest, jnp.max(scores, axis=0, keepdims=True))
                scores = scores - newest
                accum, largest = accum * jnp.exp2(largest - newest), newest
            weights = jnp.exp2(scores)
            if valid is not None:
                weights = jnp.where(valid, weights, 0.0)
            return accum + jnp.dot(values, weights.astype(BF16), preferred_element_type=F32), largest

        state = jnp.zeros((HD + 16, count), F32), jnp.full((1, count), -1e30, F32)
        tile = pick(ttiles)
        state = absorb(state, tile.reshape(HD, HD).astype(BF16), pltpu.roll(tile, TT, 1).reshape(HD, HD), valid)
        for one, other in zip(kvs[::2], kvs[1::2]):
            keys, values = [], []
            for kv in (one, other):
                keys.append(kv[:, pl.ds(at, TOK), :].reshape(block, HD))
                values.append(kv[:, pl.ds(PER * TOK + at, TOK), :].reshape(block, HD))
            state = absorb(state, jnp.concatenate(keys, axis=0), jnp.concatenate(values, axis=0), None)
        accum, largest = state
        total = accum[HD : HD + 1]
        logs = jnp.log2(total) if fast else jnp.log2(total) + largest
        mixed = (accum[:HD] / total).T.astype(BF16)
        out[h - first, :block, :] = mixed[:block]
        last = empty
        if texts:
            line = jnp.broadcast_to(logs[:, block:], (8, HD))
            last = line[:1]
            out[h - first, block:QT, :] = mixed[block : block + 16]
            for i in range(1, tiles):
                pieces = split(pltpu.roll(line, HD - 16 * i, 1)[:1])
                pieces = jnp.concatenate([*pieces, jnp.zeros((13, HD), F32)], axis=0)
                texts_out[i - 1][h - first, :16, :] = mixed[block + 16 * i : block + 16 * i + 16]
                texts_out[i - 1][h - first, 16:, :] = pieces.astype(BF16)
        elif ready:
            out[h - first, block:QT, :] = done[h, :16, :]
            pieces = done[h, 16:, :].astype(F32)
            last = pieces[0:1] + pieces[1:2] + pieces[2:3]
        else:
            out[h - first, block:QT, :] = jnp.zeros((16, HD), BF16)
        logs = jnp.concatenate([logs[:, i * HD : (i + 1) * HD] for i in range(4)] + [last], axis=0)
        out[h - first, QT:, :] = jnp.concatenate([*split(logs), empty], axis=0).astype(BF16)

    @pl.when(bounded)
    def _():
        for h in heads:
            head(h, True)

    @pl.when(jnp.logical_not(bounded))
    def _():
        @pl.loop(first, heads[-1] + 1)
        def _(h):
            head(h, False)


def combine_kernel(from3, from2, from1, early, late, text3, text0, out):
    block = GROUPS * TOK

    def rows_of(share, count):
        row = jnp.concatenate([share[i : i + 1] for i in range(share.shape[0])], axis=1)
        return jnp.broadcast_to(row, (HD, row.shape[1])).T[:count]

    def join(logs, values):
        top = functools.reduce(jnp.maximum, logs)
        shares = [jnp.exp2(l - top) for l in logs]
        total = sum(shares)
        count = values[0].shape[0]
        return sum(rows_of(share / total, count) * value.astype(F32) for share, value in zip(shares, values))

    texts = []
    for h in range(PER):
        own = early.at[h] if h < PER - 1 else late.at[0]
        parts = [from3.at[h], from2.at[h], from1.at[h], own]
        logs = []
        for part in parts:
            pieces = part[QT:, :].astype(F32)
            logs.append(pieces[0:5] + pieces[5:10] + pieces[10:15])
        mixed = join([l[:4] for l in logs], [part[:block, :] for part in parts])
        out[:, h * TOK : (h + 1) * TOK, :] = mixed.reshape(GROUPS, TOK, HD).astype(BF16)
        tlogs, tvalues = [], []
        for i, text in ((0, text3), (3, text0)):
            pieces = text[h, 16:, :].astype(F32)
            logs[i] = pieces[0:1] + pieces[1:2] + pieces[2:3]
        tlogs = [logs[0], logs[1][4:5], logs[2][4:5], logs[3]]
        tvalues = [text3[h, :16, :], parts[1][block:QT, :], parts[2][block:QT, :], text0[h, :16, :]]
        texts.append(join(tlogs, tvalues))
    for zl in range(4):
        rows = [text[zl * TT : (zl + 1) * TT] for text in texts]
        rows = jnp.concatenate(rows + [jnp.zeros((TT, HD), F32)], axis=0).astype(BF16)
        for zh in range(2):
            out[4 * zh + zl, PER * TOK :, :] = rows


def final_kernel(parts, video, text):
    for head in range(HEADS):
        group, h = divmod(head, PER)
        video[:, head * HD : (head + 1) * HD] = parts[group, h * TOK : (h + 1) * TOK, :]
    own = own_group()
    for pair in range(2):
        piece = jnp.zeros((16, HD), F32)
        for u in range(4):
            piece += jnp.where(own == u, parts[2 * u + pair, PER * TOK :, :].astype(F32), 0.0)
        for h in range(PER):
            lanes = (pair * PER + h) * HD
            text[:, lanes : lanes + HD] = piece[h * TT : (h + 1) * TT].astype(BF16)


def shift(values, axis, by):
    n = lax.axis_size(axis)
    return lax.ppermute(values, axis, [(i, (i + by) % n) for i in range(n)])


def onward(near, axis):
    n = lax.axis_size(axis)
    passed = jnp.where(lax.axis_index("c") == 0, near[0], near[1])
    moves = [(2 * i + c, 2 * ((i + (-1 if c else 1)) % n) + c) for i in range(n) for c in range(2)]
    return lax.ppermute(passed, (axis, "c"), moves)


def whole(*shapes):
    return [pl.BlockSpec(memory_space=pltpu.VMEM) for _ in shapes]


def body(
    video_q,
    video_k,
    video_v,
    text_q,
    text_k,
    text_v,
    video_q_gain,
    video_k_gain,
    text_q_gain,
    text_k_gain,
    frame_ids,
    row_ids,
    col_ids,
    text_mask,
):
    params = pltpu.CompilerParams(vmem_limit_bytes=VMEM)
    alone = pltpu.CompilerParams(vmem_limit_bytes=56 * 2**20)
    gains = [g.reshape(1, HD) for g in (video_q_gain, text_q_gain, video_k_gain, text_k_gain)]
    ids = [i.reshape(1, TOK) for i in (frame_ids, row_ids, col_ids)]
    freqs, part = lane_tables()
    spots = (part[None, :] == np.arange(8)[:, None]).astype(jnp.bfloat16)
    operands = (video_k, video_v, text_k, text_v, gains[2], gains[3], *ids, freqs.reshape(1, HD), spots)
    kv, tables = pl.pallas_call(
        prep_kv_kernel,
        out_shape=(
            jax.ShapeDtypeStruct((GROUPS, KVROWS, HD), BF16),
            jax.ShapeDtypeStruct((2, TOK, HD), F32),
        ),
        in_specs=[pl.BlockSpec(memory_space=pltpu.SMEM)] + whole(*operands),
        out_specs=tuple(whole(0, 0)),
        compiler_params=alone,
        name="prep_kv",
    )(text_mask, *operands)
    operands = (video_q, text_q, gains[0], gains[1], tables)
    q = pl.pallas_call(
        prep_q_kernel,
        out_shape=jax.ShapeDtypeStruct((GROUPS, QROWS, HD), BF16),
        in_specs=whole(*operands),
        out_specs=whole(0)[0],
        compiler_params=alone,
        name="prep_q",
    )(*operands)
    kv = lax.all_to_all(kv, Z, split_axis=0, concat_axis=0, tiled=True)
    kv, q = lax.optimization_barrier((kv, q))
    near = [shift(kv, "y", 1), shift(kv, "y", 3)]
    kvs = [kv, shift(kv, "c", 1)]
    q = lax.all_to_all(q, Z, split_axis=0, concat_axis=0, tiled=True)
    q, *near = lax.optimization_barrier((q, *near))
    far = onward(near, "y")
    tiles = {0: q, 1: shift(q, "x", 1), 3: shift(q, "x", 3)}
    for mine in (*near, far):
        kvs += [mine, shift(mine, "c", 1)]
    tiles[2] = onward([tiles[1], tiles[3]], "x")
    strength = jnp.concatenate(gains, axis=0)

    def attend(tiles, heads, done=None):
        operands = (strength, *tiles, *([] if done is None else [done]), *kvs)
        shapes = [jax.ShapeDtypeStruct((len(heads), OT, HD), BF16)]
        shapes += [jax.ShapeDtypeStruct((len(heads), 32, HD), BF16) for _ in tiles[1:]]
        return pl.pallas_call(
            functools.partial(attend_kernel, tiles=len(tiles), ready=done is not None, heads=heads),
            in_specs=whole(*operands),
            out_specs=whole(*shapes),
            out_shape=shapes,
            compiler_params=params,
            name="attend",
        )(*operands)

    tie = lax.optimization_barrier
    every = tuple(range(PER))
    (from3,) = attend([tiles[3]], every)
    tiles[2], from3 = tie((tiles[2], from3))
    from3 = shift(from3, "x", 1)
    from2, text3, text1, text0 = attend([tiles[2], tiles[3], tiles[1], tiles[0]], every)
    tile, from3, from2, text3 = tie((tiles[1], from3, from2, text3))
    from2 = shift(from2, "x", 2)
    text3 = shift(text3, "x", 1)
    (from1,) = attend([tile], every, text1)
    tile, from1 = tie((tiles[0], from1))
    from1 = shift(from1, "x", 3)
    (early,) = attend([tile], every[:-1])
    tile, from2, early = tie((tile, from2, early))
    (late,) = attend([tile], every[-1:])
    parts = (from3, from2, from1, early, late, text3, text0)
    back = pl.pallas_call(
        combine_kernel,
        out_shape=jax.ShapeDtypeStruct((GROUPS, BACK, HD), BF16),
        in_specs=whole(*parts),
        out_specs=whole(0)[0],
        compiler_params=params,
        name="combine",
    )(*parts)
    back = lax.all_to_all(back, Z, split_axis=0, concat_axis=0, tiled=True)
    return pl.pallas_call(
        final_kernel,
        out_shape=(
            jax.ShapeDtypeStruct(video_q.shape, BF16),
            jax.ShapeDtypeStruct(text_q.shape, BF16),
        ),
        in_specs=whole(0),
        out_specs=tuple(whole(0, 0)),
        compiler_params=params,
        name="final",
    )(back)


def solution(mesh):
    devices = mesh.devices.reshape(4, 4, 4, 2, 2)
    mesh = Mesh(devices, ALL)
    tokens = P(ALL, None)
    text = P(("zl", "y", "x"), ("zh", "c"))
    ids = P(ALL)
    in_specs = (tokens, tokens, tokens, text, text, text, P(), P(), P(), P(), ids, ids, ids, P(("zl", "y", "x")))
    out_specs = (tokens, text)
    return jax.shard_map(body, mesh=mesh, in_specs=in_specs, out_specs=out_specs, check_vma=False)
```

```python
import functools
import math

import jax
import jax.numpy as jnp
import numpy as np
from jax import lax
from jax.experimental import pallas as pl
from jax.experimental.pallas import tpu as pltpu
from jax.sharding import Mesh
from jax.sharding import PartitionSpec as P

HD = 128
RT = 16
RH = 56
RW = 56
HEADS = 24
GROUPS = 8
PER = HEADS // GROUPS
TOK = 64
TT = 4
KVROWS = 2 * PER * TOK + 32
QROWS = PER * TOK + 16
QT = GROUPS * TOK + 16
OT = QT + 16
BACK = PER * TOK + 16
LIMIT = 100.0
SCALE = math.log2(math.e) / math.sqrt(HD)
NT = (((1,), (1,)), ((), ()))
Z = ("zh", "zl")
ALL = ("zl", "y", "x", "zh", "c")
VMEM = 24 * 2**20
F32 = jnp.float32
BF16 = jnp.bfloat16


def lane_tables():
    freqs, part = [], []
    for number, width in enumerate((RT, RH, RW)):
        index = np.arange(width // 2, dtype=np.float32)
        freqs.append(np.power(np.float32(256.0), (-2.0 * index / width).astype(np.float32)))
        part.append(np.full((width // 2,), number))
    freqs = np.repeat(np.concatenate(freqs), 2).astype(np.float32)
    part = np.repeat(np.concatenate(part), 2)
    return freqs, part


def norm(values, gain):
    values = values.astype(F32)
    meansq = jnp.mean(values * values, axis=-1, keepdims=True)
    return values * lax.rsqrt(meansq + 1e-06) * gain


def own_group():
    return 2 * lax.axis_index("zh") + lax.axis_index("c")


def swap_pairs(lanes):
    row = lax.broadcasted_iota(jnp.int32, (lanes, lanes), 0)
    column = lax.broadcasted_iota(jnp.int32, (lanes, lanes), 1)
    return (row == column + 1 - 2 * (column % 2)).astype(F32).astype(BF16)


def turning(gain, cos, sin):
    swap = swap_pairs(HD)
    even = lax.broadcasted_iota(jnp.int32, (8, HD), 1) % 2 == 0
    wide = jnp.broadcast_to(gain, (8, HD))
    other = jnp.where(even, pltpu.roll(wide, HD - 1, 1), pltpu.roll(wide, 1, 1))[:1]
    cos, sin = cos * gain, sin * other

    def turn(values):
        swapped = jnp.dot(values, swap, preferred_element_type=F32)
        x = values.astype(F32)
        scale = lax.rsqrt(jnp.mean(x * x, axis=-1, keepdims=True) + 1e-06)
        return ((x * cos + swapped * sin) * scale).astype(BF16)

    return turn


def prep_kv_kernel(mask, k, v, tk, tv, kg, tkg, frames, rows, cols, freqs, part, kv_out, tables):
    spots = jnp.concatenate([frames[...], rows[...], cols[...], jnp.zeros((5, TOK), jnp.int32)], axis=0)
    position = lax.dot_general(
        spots.astype(F32).astype(BF16), part[...], (((0,), (0,)), ((), ())), preferred_element_type=F32
    )
    angle = position * freqs[...]
    lane = lax.broadcasted_iota(jnp.int32, (TOK, HD), 1)
    cos = jnp.cos(angle)
    sin = jnp.sin(angle)
    sin = jnp.where(lane % 2 == 0, -sin, sin)
    tables[0] = cos
    tables[1] = sin
    turn = turning(kg[...], cos, sin)
    for head in range(HEADS):
        group, h = divmod(head, PER)
        lanes = slice(head * HD, (head + 1) * HD)
        kv_out[group, h * TOK : (h + 1) * TOK, :] = turn(k[:, lanes])
        kv_out[group, (PER + h) * TOK : (PER + h + 1) * TOK, :] = v[:, lanes]
    own = own_group()
    tks, tvs = tk[...].astype(F32), tv[...].astype(F32)
    token = lax.broadcasted_iota(jnp.int32, (2 * TT, HD), 0)
    last = jnp.zeros((2 * TT, HD), F32)
    for t in range(TT):
        last = jnp.where(token == t, mask[t].astype(F32), last)
    for pair in range(2):
        krows = []
        for h in range(PER):
            lanes = slice((pair * PER + h) * HD, (pair * PER + h + 1) * HD)
            krows.append(norm(tks[:, lanes], tkg[...]))
            krows.append(tvs[:, lanes])
        krows = jnp.concatenate(krows + [last], axis=0)
        for group in range(pair, GROUPS, 2):
            kv_out[group, 2 * PER * TOK :, :] = jnp.where(own == group // 2, krows, 0.0).astype(BF16)


def prep_q_kernel(q, tq, qg, tqg, tables, q_out):
    turn = turning(qg[...], tables[0], tables[1])
    for head in range(HEADS):
        group, h = divmod(head, PER)
        lanes = slice(head * HD, (head + 1) * HD)
        q_out[group, h * TOK : (h + 1) * TOK, :] = turn(q[:, lanes])
    own = own_group()
    tqs = tq[...].astype(F32)
    for pair in range(2):
        qrows = []
        for h in range(PER):
            lanes = slice((pair * PER + h) * HD, (pair * PER + h + 1) * HD)
            qrows.append(norm(tqs[:, lanes], tqg[...]))
        qrows = jnp.concatenate(qrows + [jnp.zeros((TT, HD), F32)], axis=0)
        for group in range(pair, GROUPS, 2):
            q_out[group, PER * TOK :, :] = jnp.where(own == group // 2, qrows, 0.0).astype(BF16)


def text_queries(tile):
    upper = lax.broadcasted_iota(jnp.int32, (2, 8, HD), 1) < TT

    def pairs(rows, low):
        rows = rows.reshape(2, 2, 8, HD)
        one, other = rows[:, 0], rows[:, 1]
        if low:
            return jnp.where(upper, one, pltpu.roll(other, TT, 1)).reshape(16, HD)
        return jnp.where(upper, pltpu.roll(one, TT, 1), other).reshape(16, HD)

    rows = tile[:, PER * TOK :, :].astype(F32)
    rows = rows[:4] + rows[4:]
    return pairs(rows[:, :8], True), pairs(rows[:, :8], False), pairs(rows[:, 8:], True)


def split(logs):
    high = logs.astype(BF16).astype(F32)
    middle = (logs - high).astype(BF16).astype(F32)
    return high, middle, logs - high - middle


def attend_kernel(gains, *refs, tiles, ready, heads):
    queries_in, refs = refs[:tiles], refs[tiles:]
    if ready:
        done, refs = refs[0], refs[1:]
    if tiles > 1:
        refs, texts_out = refs[: 1 - tiles], refs[1 - tiles :]
    kvs, out = refs[:-1], refs[-1]
    first = heads[0]
    block = GROUPS * TOK
    texts = [text_queries(q) for q in queries_in] if tiles > 1 else []
    empty = jnp.zeros((1, HD), F32)

    both = []
    for one, other in zip(kvs[::2], kvs[1::2]):
        tile = one[:, 2 * PER * TOK :, :].astype(F32) + other[:, 2 * PER * TOK :, :].astype(F32)
        both.append(tile[:4] + tile[4:])
    both = jnp.concatenate(both, axis=0)
    ttiles = [both[:, 8 * h : 8 * h + 8] for h in range(PER)]
    valid = both[:, 24:32].reshape(HD, HD)[:, :1] > 0.0

    strongest = jnp.max(jnp.abs(gains[...]), axis=1, keepdims=True)
    reach = jnp.max(strongest[0:2]) * jnp.max(strongest[2:4]) * (HD * SCALE * 1.01)
    bounded = reach <= LIMIT

    def head(h, fast):
        at = h * TOK if isinstance(h, int) else pl.multiple_of(h * TOK, TOK)

        def pick(three):
            if isinstance(h, int):
                return three[h]
            return jnp.where(h == 0, three[0], jnp.where(h == 1, three[1], three[2]))

        queries = queries_in[0][:, pl.ds(at, TOK), :].reshape(block, HD)
        if texts:
            rows = [pick(text) for text in texts] + [jnp.zeros((HD - 16 * tiles, HD), F32)]
            queries = jnp.concatenate([queries, jnp.concatenate(rows, axis=0).astype(BF16)], axis=0)
        count = queries.shape[0]

        def absorb(state, keys, values, valid):
            accum, largest = state
            scores = lax.dot_general(keys, queries, NT, preferred_element_type=F32) * SCALE
            values = jnp.concatenate([values.astype(F32).T.astype(BF16), jnp.ones((16, values.shape[0]), BF16)], axis=0)
            if not fast:
                if valid is not None:
                    scores = jnp.where(valid, scores, -1e30)
                newest = jnp.maximum(largest, jnp.max(scores, axis=0, keepdims=True))
                scores = scores - newest
                accum, largest = accum * jnp.exp2(largest - newest), newest
            weights = jnp.exp2(scores)
            if valid is not None:
                weights = jnp.where(valid, weights, 0.0)
            return accum + jnp.dot(values, weights.astype(BF16), preferred_element_type=F32), largest

        state = jnp.zeros((HD + 16, count), F32), jnp.full((1, count), -1e30, F32)
        tile = pick(ttiles)
        state = absorb(state, tile.reshape(HD, HD).astype(BF16), pltpu.roll(tile, TT, 1).reshape(HD, HD), valid)
        for one, other in zip(kvs[::2], kvs[1::2]):
            keys, values = [], []
            for kv in (one, other):
                keys.append(kv[:, pl.ds(at, TOK), :].reshape(block, HD))
                values.append(kv[:, pl.ds(PER * TOK + at, TOK), :].reshape(block, HD))
            state = absorb(state, jnp.concatenate(keys, axis=0), jnp.concatenate(values, axis=0), None)
        accum, largest = state
        total = accum[HD : HD + 1]
        logs = jnp.log2(total) if fast else jnp.log2(total) + largest
        mixed = (accum[:HD] / total).T.astype(BF16)
        out[h - first, :block, :] = mixed[:block]
        last = empty
        if texts:
            line = jnp.broadcast_to(logs[:, block:], (8, HD))
            last = line[:1]
            out[h - first, block:QT, :] = mixed[block : block + 16]
            for i in range(1, tiles):
                pieces = split(pltpu.roll(line, HD - 16 * i, 1)[:1])
                pieces = jnp.concatenate([*pieces, jnp.zeros((13, HD), F32)], axis=0)
                texts_out[i - 1][h - first, :16, :] = mixed[block + 16 * i : block + 16 * i + 16]
                texts_out[i - 1][h - first, 16:, :] = pieces.astype(BF16)
        elif ready:
            out[h - first, block:QT, :] = done[h, :16, :]
            pieces = done[h, 16:, :].astype(F32)
            last = pieces[0:1] + pieces[1:2] + pieces[2:3]
        else:
            out[h - first, block:QT, :] = jnp.zeros((16, HD), BF16)
        logs = jnp.concatenate([logs[:, i * HD : (i + 1) * HD] for i in range(4)] + [last], axis=0)
        out[h - first, QT:, :] = jnp.concatenate([*split(logs), empty], axis=0).astype(BF16)

    @pl.when(bounded)
    def _():
        for h in heads:
            head(h, True)

    @pl.when(jnp.logical_not(bounded))
    def _():
        @pl.loop(first, heads[-1] + 1)
        def _(h):
            head(h, False)


def combine_kernel(from3, from2, from1, early, late, text3, text0, out):
    block = GROUPS * TOK

    def rows_of(share, count):
        row = jnp.concatenate([share[i : i + 1] for i in range(share.shape[0])], axis=1)
        return jnp.broadcast_to(row, (HD, row.shape[1])).T[:count]

    def join(logs, values):
        top = functools.reduce(jnp.maximum, logs)
        shares = [jnp.exp2(l - top) for l in logs]
        total = sum(shares)
        count = values[0].shape[0]
        return sum(rows_of(share / total, count) * value.astype(F32) for share, value in zip(shares, values))

    texts = []
    for h in range(PER):
        own = early.at[h] if h < PER - 1 else late.at[0]
        parts = [from3.at[h], from2.at[h], from1.at[h], own]
        logs = []
        for part in parts:
            pieces = part[QT:, :].astype(F32)
            logs.append(pieces[0:5] + pieces[5:10] + pieces[10:15])
        mixed = join([l[:4] for l in logs], [part[:block, :] for part in parts])
        out[:, h * TOK : (h + 1) * TOK, :] = mixed.reshape(GROUPS, TOK, HD).astype(BF16)
        tlogs, tvalues = [], []
        for i, text in ((0, text3), (3, text0)):
            pieces = text[h, 16:, :].astype(F32)
            logs[i] = pieces[0:1] + pieces[1:2] + pieces[2:3]
        tlogs = [logs[0], logs[1][4:5], logs[2][4:5], logs[3]]
        tvalues = [text3[h, :16, :], parts[1][block:QT, :], parts[2][block:QT, :], text0[h, :16, :]]
        texts.append(join(tlogs, tvalues))
    for zl in range(4):
        rows = [text[zl * TT : (zl + 1) * TT] for text in texts]
        rows = jnp.concatenate(rows + [jnp.zeros((TT, HD), F32)], axis=0).astype(BF16)
        for zh in range(2):
            out[4 * zh + zl, PER * TOK :, :] = rows


def final_kernel(parts, video, text):
    for head in range(HEADS):
        group, h = divmod(head, PER)
        video[:, head * HD : (head + 1) * HD] = parts[group, h * TOK : (h + 1) * TOK, :]
    own = own_group()
    for pair in range(2):
        piece = jnp.zeros((16, HD), F32)
        for u in range(4):
            piece += jnp.where(own == u, parts[2 * u + pair, PER * TOK :, :].astype(F32), 0.0)
        for h in range(PER):
            lanes = (pair * PER + h) * HD
            text[:, lanes : lanes + HD] = piece[h * TT : (h + 1) * TT].astype(BF16)


def shift(values, axis, by):
    n = lax.axis_size(axis)
    return lax.ppermute(values, axis, [(i, (i + by) % n) for i in range(n)])


def onward(near, axis):
    n = lax.axis_size(axis)
    passed = jnp.where(lax.axis_index("c") == 0, near[0], near[1])
    moves = [(2 * i + c, 2 * ((i + (-1 if c else 1)) % n) + c) for i in range(n) for c in range(2)]
    return lax.ppermute(passed, (axis, "c"), moves)


def whole(*shapes):
    return [pl.BlockSpec(memory_space=pltpu.VMEM) for _ in shapes]


def body(
    video_q,
    video_k,
    video_v,
    text_q,
    text_k,
    text_v,
    video_q_gain,
    video_k_gain,
    text_q_gain,
    text_k_gain,
    frame_ids,
    row_ids,
    col_ids,
    text_mask,
):
    params = pltpu.CompilerParams(vmem_limit_bytes=VMEM)
    alone = pltpu.CompilerParams(vmem_limit_bytes=56 * 2**20)
    gains = [g.reshape(1, HD) for g in (video_q_gain, text_q_gain, video_k_gain, text_k_gain)]
    ids = [i.reshape(1, TOK) for i in (frame_ids, row_ids, col_ids)]
    freqs, part = lane_tables()
    spots = (part[None, :] == np.arange(8)[:, None]).astype(jnp.bfloat16)
    operands = (video_k, video_v, text_k, text_v, gains[2], gains[3], *ids, freqs.reshape(1, HD), spots)
    kv, tables = pl.pallas_call(
        prep_kv_kernel,
        out_shape=(
            jax.ShapeDtypeStruct((GROUPS, KVROWS, HD), BF16),
            jax.ShapeDtypeStruct((2, TOK, HD), F32),
        ),
        in_specs=[pl.BlockSpec(memory_space=pltpu.SMEM)] + whole(*operands),
        out_specs=tuple(whole(0, 0)),
        compiler_params=alone,
        name="prep_kv",
    )(text_mask, *operands)
    operands = (video_q, text_q, gains[0], gains[1], tables)
    q = pl.pallas_call(
        prep_q_kernel,
        out_shape=jax.ShapeDtypeStruct((GROUPS, QROWS, HD), BF16),
        in_specs=whole(*operands),
        out_specs=whole(0)[0],
        compiler_params=alone,
        name="prep_q",
    )(*operands)
    kv = lax.all_to_all(kv, Z, split_axis=0, concat_axis=0, tiled=True)
    kv, q = lax.optimization_barrier((kv, q))
    near = [shift(kv, "y", 1), shift(kv, "y", 3)]
    kvs = [kv, shift(kv, "c", 1)]
    q = lax.all_to_all(q, Z, split_axis=0, concat_axis=0, tiled=True)
    q, *near = lax.optimization_barrier((q, *near))
    far = onward(near, "y")
    tiles = {0: q, 1: shift(q, "x", 1), 3: shift(q, "x", 3)}
    for mine in (*near, far):
        kvs += [mine, shift(mine, "c", 1)]
    tiles[2] = onward([tiles[1], tiles[3]], "x")
    strength = jnp.concatenate(gains, axis=0)

    def attend(tiles, heads, done=None):
        operands = (strength, *tiles, *([] if done is None else [done]), *kvs)
        shapes = [jax.ShapeDtypeStruct((len(heads), OT, HD), BF16)]
        shapes += [jax.ShapeDtypeStruct((len(heads), 32, HD), BF16) for _ in tiles[1:]]
        return pl.pallas_call(
            functools.partial(attend_kernel, tiles=len(tiles), ready=done is not None, heads=heads),
            in_specs=whole(*operands),
            out_specs=whole(*shapes),
            out_shape=shapes,
            compiler_params=params,
            name="attend",
        )(*operands)

    tie = lax.optimization_barrier
    every = tuple(range(PER))
    (from3,) = attend([tiles[3]], every)
    tiles[2], from3 = tie((tiles[2], from3))
    from3 = shift(from3, "x", 1)
    from2, text3, text1, text0 = attend([tiles[2], tiles[3], tiles[1], tiles[0]], every)
    tile, from2, text3 = tie((tiles[1], from2, text3))
    from2 = shift(from2, "x", 2)
    text3 = shift(text3, "x", 1)
    (from1,) = attend([tile], every, text1)
    tile, from1 = tie((tiles[0], from1))
    from1 = shift(from1, "x", 3)
    tile, from3 = tie((tile, from3))
    (early,) = attend([tile], every[:-1])
    tile, from2, early = tie((tile, from2, early))
    (late,) = attend([tile], every[-1:])
    parts = (from3, from2, from1, early, late, text3, text0)
    back = pl.pallas_call(
        combine_kernel,
        out_shape=jax.ShapeDtypeStruct((GROUPS, BACK, HD), BF16),
        in_specs=whole(*parts),
        out_specs=whole(0)[0],
        compiler_params=params,
        name="combine",
    )(*parts)
    back = lax.all_to_all(back, Z, split_axis=0, concat_axis=0, tiled=True)
    return pl.pallas_call(
        final_kernel,
        out_shape=(
            jax.ShapeDtypeStruct(video_q.shape, BF16),
            jax.ShapeDtypeStruct(text_q.shape, BF16),
        ),
        in_specs=whole(0),
        out_specs=tuple(whole(0, 0)),
        compiler_params=params,
        name="final",
    )(back)


def solution(mesh):
    devices = mesh.devices.reshape(4, 4, 4, 2, 2)
    mesh = Mesh(devices, ALL)
    tokens = P(ALL, None)
    text = P(("zl", "y", "x"), ("zh", "c"))
    ids = P(ALL)
    in_specs = (tokens, tokens, tokens, text, text, text, P(), P(), P(), P(), ids, ids, ids, P(("zl", "y", "x")))
    out_specs = (tokens, text)
    return jax.shard_map(body, mesh=mesh, in_specs=in_specs, out_specs=out_specs, check_vma=False)
```

```python
import functools
import math

import jax
import jax.numpy as jnp
import numpy as np
from jax import lax
from jax.experimental import pallas as pl
from jax.experimental.pallas import tpu as pltpu
from jax.sharding import Mesh
from jax.sharding import PartitionSpec as P

HD = 128
RT = 16
RH = 56
RW = 56
HEADS = 24
GROUPS = 8
PER = HEADS // GROUPS
TOK = 64
TT = 4
KVROWS = 2 * PER * TOK + 32
QROWS = PER * TOK + 16
QT = GROUPS * TOK + 16
OT = QT + 16
BACK = PER * TOK + 16
LIMIT = 100.0
SCALE = math.log2(math.e) / math.sqrt(HD)
NT = (((1,), (1,)), ((), ()))
Z = ("zh", "zl")
ALL = ("zl", "y", "x", "zh", "c")
VMEM = 24 * 2**20
F32 = jnp.float32
BF16 = jnp.bfloat16


def lane_tables():
    freqs, part = [], []
    for number, width in enumerate((RT, RH, RW)):
        index = np.arange(width // 2, dtype=np.float32)
        freqs.append(np.power(np.float32(256.0), (-2.0 * index / width).astype(np.float32)))
        part.append(np.full((width // 2,), number))
    freqs = np.repeat(np.concatenate(freqs), 2).astype(np.float32)
    part = np.repeat(np.concatenate(part), 2)
    return freqs, part


def norm(values, gain):
    values = values.astype(F32)
    meansq = jnp.mean(values * values, axis=-1, keepdims=True)
    return values * lax.rsqrt(meansq + 1e-06) * gain


def own_group():
    return 2 * lax.axis_index("zh") + lax.axis_index("c")


def swap_pairs(lanes):
    row = lax.broadcasted_iota(jnp.int32, (lanes, lanes), 0)
    column = lax.broadcasted_iota(jnp.int32, (lanes, lanes), 1)
    return (row == column + 1 - 2 * (column % 2)).astype(F32).astype(BF16)


def turning(gain, cos, sin):
    swap = swap_pairs(HD)
    even = lax.broadcasted_iota(jnp.int32, (8, HD), 1) % 2 == 0
    wide = jnp.broadcast_to(gain, (8, HD))
    other = jnp.where(even, pltpu.roll(wide, HD - 1, 1), pltpu.roll(wide, 1, 1))[:1]
    cos, sin = cos * gain, sin * other

    def turn(values):
        swapped = jnp.dot(values, swap, preferred_element_type=F32)
        x = values.astype(F32)
        scale = lax.rsqrt(jnp.mean(x * x, axis=-1, keepdims=True) + 1e-06)
        return ((x * cos + swapped * sin) * scale).astype(BF16)

    return turn


def prep_kv_kernel(mask, k, v, tk, tv, kg, tkg, frames, rows, cols, freqs, part, kv_out, tables):
    spots = jnp.concatenate([frames[...], rows[...], cols[...], jnp.zeros((5, TOK), jnp.int32)], axis=0)
    position = lax.dot_general(
        spots.astype(F32).astype(BF16), part[...], (((0,), (0,)), ((), ())), preferred_element_type=F32
    )
    angle = position * freqs[...]
    lane = lax.broadcasted_iota(jnp.int32, (TOK, HD), 1)
    cos = jnp.cos(angle)
    sin = jnp.sin(angle)
    sin = jnp.where(lane % 2 == 0, -sin, sin)
    tables[0] = cos
    tables[1] = sin
    turn = turning(kg[...], cos, sin)
    for head in range(HEADS):
        group, h = divmod(head, PER)
        lanes = slice(head * HD, (head + 1) * HD)
        kv_out[group, h * TOK : (h + 1) * TOK, :] = turn(k[:, lanes])
        kv_out[group, (PER + h) * TOK : (PER + h + 1) * TOK, :] = v[:, lanes]
    own = own_group()
    tks, tvs = tk[...].astype(F32), tv[...].astype(F32)
    token = lax.broadcasted_iota(jnp.int32, (2 * TT, HD), 0)
    last = jnp.zeros((2 * TT, HD), F32)
    for t in range(TT):
        last = jnp.where(token == t, mask[t].astype(F32), last)
    for pair in range(2):
        krows = []
        for h in range(PER):
            lanes = slice((pair * PER + h) * HD, (pair * PER + h + 1) * HD)
            krows.append(norm(tks[:, lanes], tkg[...]))
            krows.append(tvs[:, lanes])
        krows = jnp.concatenate(krows + [last], axis=0)
        for group in range(pair, GROUPS, 2):
            kv_out[group, 2 * PER * TOK :, :] = jnp.where(own == group // 2, krows, 0.0).astype(BF16)


def prep_q_kernel(q, tq, qg, tqg, tables, q_out):
    turn = turning(qg[...], tables[0], tables[1])
    for head in range(HEADS):
        group, h = divmod(head, PER)
        lanes = slice(head * HD, (head + 1) * HD)
        q_out[group, h * TOK : (h + 1) * TOK, :] = turn(q[:, lanes])
    own = own_group()
    tqs = tq[...].astype(F32)
    for pair in range(2):
        qrows = []
        for h in range(PER):
            lanes = slice((pair * PER + h) * HD, (pair * PER + h + 1) * HD)
            qrows.append(norm(tqs[:, lanes], tqg[...]))
        qrows = jnp.concatenate(qrows + [jnp.zeros((TT, HD), F32)], axis=0)
        for group in range(pair, GROUPS, 2):
            q_out[group, PER * TOK :, :] = jnp.where(own == group // 2, qrows, 0.0).astype(BF16)


def text_queries(tile):
    upper = lax.broadcasted_iota(jnp.int32, (2, 8, HD), 1) < TT

    def pairs(rows, low):
        rows = rows.reshape(2, 2, 8, HD)
        one, other = rows[:, 0], rows[:, 1]
        if low:
            return jnp.where(upper, one, pltpu.roll(other, TT, 1)).reshape(16, HD)
        return jnp.where(upper, pltpu.roll(one, TT, 1), other).reshape(16, HD)

    rows = tile[:, PER * TOK :, :].astype(F32)
    rows = rows[:4] + rows[4:]
    return pairs(rows[:, :8], True), pairs(rows[:, :8], False), pairs(rows[:, 8:], True)


def split(logs):
    high = logs.astype(BF16).astype(F32)
    middle = (logs - high).astype(BF16).astype(F32)
    return high, middle, logs - high - middle


def attend_kernel(gains, *refs, tiles, ready, heads):
    queries_in, refs = refs[:tiles], refs[tiles:]
    if ready:
        done, refs = refs[0], refs[1:]
    if tiles > 1:
        refs, texts_out = refs[: 1 - tiles], refs[1 - tiles :]
    kvs, out = refs[:-1], refs[-1]
    first = heads[0]
    block = GROUPS * TOK
    texts = [text_queries(q) for q in queries_in] if tiles > 1 else []
    empty = jnp.zeros((1, HD), F32)

    both = []
    for one, other in zip(kvs[::2], kvs[1::2]):
        tile = one[:, 2 * PER * TOK :, :].astype(F32) + other[:, 2 * PER * TOK :, :].astype(F32)
        both.append(tile[:4] + tile[4:])
    both = jnp.concatenate(both, axis=0)
    ttiles = [both[:, 8 * h : 8 * h + 8] for h in range(PER)]
    valid = both[:, 24:32].reshape(HD, HD)[:, :1] > 0.0

    strongest = jnp.max(jnp.abs(gains[...]), axis=1, keepdims=True)
    reach = jnp.max(strongest[0:2]) * jnp.max(strongest[2:4]) * (HD * SCALE * 1.01)
    bounded = reach <= LIMIT

    def head(h, fast):
        at = h * TOK if isinstance(h, int) else pl.multiple_of(h * TOK, TOK)

        def pick(three):
            if isinstance(h, int):
                return three[h]
            return jnp.where(h == 0, three[0], jnp.where(h == 1, three[1], three[2]))

        queries = queries_in[0][:, pl.ds(at, TOK), :].reshape(block, HD)
        if texts:
            rows = [pick(text) for text in texts] + [jnp.zeros((HD - 16 * tiles, HD), F32)]
            queries = jnp.concatenate([queries, jnp.concatenate(rows, axis=0).astype(BF16)], axis=0)
        count = queries.shape[0]

        def absorb(state, keys, values, valid):
            accum, largest = state
            scores = lax.dot_general(keys, queries, NT, preferred_element_type=F32) * SCALE
            values = jnp.concatenate([values.astype(F32).T.astype(BF16), jnp.ones((16, values.shape[0]), BF16)], axis=0)
            if not fast:
                if valid is not None:
                    scores = jnp.where(valid, scores, -1e30)
                newest = jnp.maximum(largest, jnp.max(scores, axis=0, keepdims=True))
                scores = scores - newest
                accum, largest = accum * jnp.exp2(largest - newest), newest
            weights = jnp.exp2(scores)
            if valid is not None:
                weights = jnp.where(valid, weights, 0.0)
            return accum + jnp.dot(values, weights.astype(BF16), preferred_element_type=F32), largest

        state = jnp.zeros((HD + 16, count), F32), jnp.full((1, count), -1e30, F32)
        tile = pick(ttiles)
        state = absorb(state, tile.reshape(HD, HD).astype(BF16), pltpu.roll(tile, TT, 1).reshape(HD, HD), valid)
        for one, other in zip(kvs[::2], kvs[1::2]):
            keys, values = [], []
            for kv in (one, other):
                keys.append(kv[:, pl.ds(at, TOK), :].reshape(block, HD))
                values.append(kv[:, pl.ds(PER * TOK + at, TOK), :].reshape(block, HD))
            state = absorb(state, jnp.concatenate(keys, axis=0), jnp.concatenate(values, axis=0), None)
        accum, largest = state
        total = accum[HD : HD + 1]
        logs = jnp.log2(total) if fast else jnp.log2(total) + largest
        mixed = (accum[:HD] / total).T.astype(BF16)
        out[h - first, :block, :] = mixed[:block]
        last = empty
        if texts:
            line = jnp.broadcast_to(logs[:, block:], (8, HD))
            last = line[:1]
            out[h - first, block:QT, :] = mixed[block : block + 16]
            for i in range(1, tiles):
                pieces = split(pltpu.roll(line, HD - 16 * i, 1)[:1])
                pieces = jnp.concatenate([*pieces, jnp.zeros((13, HD), F32)], axis=0)
                texts_out[i - 1][h - first, :16, :] = mixed[block + 16 * i : block + 16 * i + 16]
                texts_out[i - 1][h - first, 16:, :] = pieces.astype(BF16)
        elif ready:
            out[h - first, block:QT, :] = done[h, :16, :]
            pieces = done[h, 16:, :].astype(F32)
            last = pieces[0:1] + pieces[1:2] + pieces[2:3]
        else:
            out[h - first, block:QT, :] = jnp.zeros((16, HD), BF16)
        logs = jnp.concatenate([logs[:, i * HD : (i + 1) * HD] for i in range(4)] + [last], axis=0)
        out[h - first, QT:, :] = jnp.concatenate([*split(logs), empty], axis=0).astype(BF16)

    @pl.when(bounded)
    def _():
        for h in heads:
            head(h, True)

    @pl.when(jnp.logical_not(bounded))
    def _():
        @pl.loop(first, heads[-1] + 1)
        def _(h):
            head(h, False)


def combine_kernel(from3, from2, from1, early, late, text3, text0, out):
    block = GROUPS * TOK

    def rows_of(share, count):
        row = jnp.concatenate([share[i : i + 1] for i in range(share.shape[0])], axis=1)
        return jnp.broadcast_to(row, (HD, row.shape[1])).T[:count]

    def join(logs, values):
        top = functools.reduce(jnp.maximum, logs)
        shares = [jnp.exp2(l - top) for l in logs]
        total = sum(shares)
        count = values[0].shape[0]
        return sum(rows_of(share / total, count) * value.astype(F32) for share, value in zip(shares, values))

    texts = []
    for h in range(PER):
        own = early.at[0] if h == 0 else late.at[h - 1]
        parts = [from3.at[h], from2.at[h], from1.at[h], own]
        logs = []
        for part in parts:
            pieces = part[QT:, :].astype(F32)
            logs.append(pieces[0:5] + pieces[5:10] + pieces[10:15])
        mixed = join([l[:4] for l in logs], [part[:block, :] for part in parts])
        out[:, h * TOK : (h + 1) * TOK, :] = mixed.reshape(GROUPS, TOK, HD).astype(BF16)
        tlogs, tvalues = [], []
        for i, text in ((0, text3), (3, text0)):
            pieces = text[h, 16:, :].astype(F32)
            logs[i] = pieces[0:1] + pieces[1:2] + pieces[2:3]
        tlogs = [logs[0], logs[1][4:5], logs[2][4:5], logs[3]]
        tvalues = [text3[h, :16, :], parts[1][block:QT, :], parts[2][block:QT, :], text0[h, :16, :]]
        texts.append(join(tlogs, tvalues))
    for zl in range(4):
        rows = [text[zl * TT : (zl + 1) * TT] for text in texts]
        rows = jnp.concatenate(rows + [jnp.zeros((TT, HD), F32)], axis=0).astype(BF16)
        for zh in range(2):
            out[4 * zh + zl, PER * TOK :, :] = rows


def final_kernel(parts, video, text):
    for head in range(HEADS):
        group, h = divmod(head, PER)
        video[:, head * HD : (head + 1) * HD] = parts[group, h * TOK : (h + 1) * TOK, :]
    own = own_group()
    for pair in range(2):
        piece = jnp.zeros((16, HD), F32)
        for u in range(4):
            piece += jnp.where(own == u, parts[2 * u + pair, PER * TOK :, :].astype(F32), 0.0)
        for h in range(PER):
            lanes = (pair * PER + h) * HD
            text[:, lanes : lanes + HD] = piece[h * TT : (h + 1) * TT].astype(BF16)


def shift(values, axis, by):
    n = lax.axis_size(axis)
    return lax.ppermute(values, axis, [(i, (i + by) % n) for i in range(n)])


def onward(near, axis):
    n = lax.axis_size(axis)
    passed = jnp.where(lax.axis_index("c") == 0, near[0], near[1])
    moves = [(2 * i + c, 2 * ((i + (-1 if c else 1)) % n) + c) for i in range(n) for c in range(2)]
    return lax.ppermute(passed, (axis, "c"), moves)


def whole(*shapes):
    return [pl.BlockSpec(memory_space=pltpu.VMEM) for _ in shapes]


def body(
    video_q,
    video_k,
    video_v,
    text_q,
    text_k,
    text_v,
    video_q_gain,
    video_k_gain,
    text_q_gain,
    text_k_gain,
    frame_ids,
    row_ids,
    col_ids,
    text_mask,
):
    params = pltpu.CompilerParams(vmem_limit_bytes=VMEM)
    alone = pltpu.CompilerParams(vmem_limit_bytes=56 * 2**20)
    gains = [g.reshape(1, HD) for g in (video_q_gain, text_q_gain, video_k_gain, text_k_gain)]
    ids = [i.reshape(1, TOK) for i in (frame_ids, row_ids, col_ids)]
    freqs, part = lane_tables()
    spots = (part[None, :] == np.arange(8)[:, None]).astype(jnp.bfloat16)
    operands = (video_k, video_v, text_k, text_v, gains[2], gains[3], *ids, freqs.reshape(1, HD), spots)
    kv, tables = pl.pallas_call(
        prep_kv_kernel,
        out_shape=(
            jax.ShapeDtypeStruct((GROUPS, KVROWS, HD), BF16),
            jax.ShapeDtypeStruct((2, TOK, HD), F32),
        ),
        in_specs=[pl.BlockSpec(memory_space=pltpu.SMEM)] + whole(*operands),
        out_specs=tuple(whole(0, 0)),
        compiler_params=alone,
        name="prep_kv",
    )(text_mask, *operands)
    operands = (video_q, text_q, gains[0], gains[1], tables)
    q = pl.pallas_call(
        prep_q_kernel,
        out_shape=jax.ShapeDtypeStruct((GROUPS, QROWS, HD), BF16),
        in_specs=whole(*operands),
        out_specs=whole(0)[0],
        compiler_params=alone,
        name="prep_q",
    )(*operands)
    kv = lax.all_to_all(kv, Z, split_axis=0, concat_axis=0, tiled=True)
    kv, q = lax.optimization_barrier((kv, q))
    near = [shift(kv, "y", 1), shift(kv, "y", 3)]
    kvs = [kv, shift(kv, "c", 1)]
    q = lax.all_to_all(q, Z, split_axis=0, concat_axis=0, tiled=True)
    q, *near = lax.optimization_barrier((q, *near))
    far = onward(near, "y")
    tiles = {0: q, 1: shift(q, "x", 1), 3: shift(q, "x", 3)}
    for mine in (*near, far):
        kvs += [mine, shift(mine, "c", 1)]
    tiles[2] = onward([tiles[1], tiles[3]], "x")
    strength = jnp.concatenate(gains, axis=0)

    def attend(tiles, heads, done=None):
        operands = (strength, *tiles, *([] if done is None else [done]), *kvs)
        shapes = [jax.ShapeDtypeStruct((len(heads), OT, HD), BF16)]
        shapes += [jax.ShapeDtypeStruct((len(heads), 32, HD), BF16) for _ in tiles[1:]]
        return pl.pallas_call(
            functools.partial(attend_kernel, tiles=len(tiles), ready=done is not None, heads=heads),
            in_specs=whole(*operands),
            out_specs=whole(*shapes),
            out_shape=shapes,
            compiler_params=params,
            name="attend",
        )(*operands)

    tie = lax.optimization_barrier
    every = tuple(range(PER))
    (from3,) = attend([tiles[3]], every)
    tiles[2], from3 = tie((tiles[2], from3))
    from3 = shift(from3, "x", 1)
    from2, text3, text1, text0 = attend([tiles[2], tiles[3], tiles[1], tiles[0]], every)
    tile, from2, text3 = tie((tiles[1], from2, text3))
    from2 = shift(from2, "x", 2)
    text3 = shift(text3, "x", 1)
    (from1,) = attend([tile], every, text1)
    tile, from1 = tie((tiles[0], from1))
    from1 = shift(from1, "x", 3)
    tile, from3 = tie((tile, from3))
    (early,) = attend([tile], every[:1])
    tile, from2, early = tie((tile, from2, early))
    (late,) = attend([tile], every[1:])
    parts = (from3, from2, from1, early, late, text3, text0)
    back = pl.pallas_call(
        combine_kernel,
        out_shape=jax.ShapeDtypeStruct((GROUPS, BACK, HD), BF16),
        in_specs=whole(*parts),
        out_specs=whole(0)[0],
        compiler_params=params,
        name="combine",
    )(*parts)
    back = lax.all_to_all(back, Z, split_axis=0, concat_axis=0, tiled=True)
    return pl.pallas_call(
        final_kernel,
        out_shape=(
            jax.ShapeDtypeStruct(video_q.shape, BF16),
            jax.ShapeDtypeStruct(text_q.shape, BF16),
        ),
        in_specs=whole(0),
        out_specs=tuple(whole(0, 0)),
        compiler_params=params,
        name="final",
    )(back)


def solution(mesh):
    devices = mesh.devices.reshape(4, 4, 4, 2, 2)
    mesh = Mesh(devices, ALL)
    tokens = P(ALL, None)
    text = P(("zl", "y", "x"), ("zh", "c"))
    ids = P(ALL)
    in_specs = (tokens, tokens, tokens, text, text, text, P(), P(), P(), P(), ids, ids, ids, P(("zl", "y", "x")))
    out_specs = (tokens, text)
    return jax.shard_map(body, mesh=mesh, in_specs=in_specs, out_specs=out_specs, check_vma=False)
```
